256 devices in a mesh: feat: 8 (over z_hi, y), node: 32 (over x, z_lo, core).
Axes of the slice: x: 4, y: 4, z: 8 (z_hi: 2, z_lo: 4; z = z_hi * 4 + z_lo), core: 2. Of those that a mesh axis runs over, the one named last changes fastest.
Arguments:
- features: bfloat16 [65536, 4096], P('node', 'feat'), may hold values from -6 to 6
- seed_feats: bfloat16 [4096, 4096], P('node', 'feat'), may hold values from -6 to 6
- patterns: int32 [1024, 8, 128, 8], P('node'), may hold values from 0 to 65535, as said below
- sources: int32 [1024, 8], P('node'), may hold values from 0 to 15
- counts: int32 [1024], P('node'), may hold values from 1 to 8
- w_self: bfloat16 [4096, 1024], P('feat'), may hold values from -0.09375 to 0.09375
- w_neigh: bfloat16 [4096, 1024], P('feat'), may hold values from -0.09375 to 0.09375
- bias_term: float32 [1024], replicated, may hold values from -3 to 3
- out_grad: bfloat16 [4096, 1024], P('node'), may hold values from -0.3125 to 0.3125
Outputs:
- hidden: bfloat16 [4096, 1024], P('node')
- grad_self: float32 [4096, 1024], P(('feat', 'node'))
- grad_neigh: float32 [4096, 1024], P(('feat', 'node'))
- grad_bias: float32 [1024], P('node')
The draws below stay inside these ranges and needn't reach their ends.
Inputs may be any that keep to these rules, and one draw needn't show every extreme that they name: `patterns`: each word holds 16 entries of 0 or 1 in its 16 low bits.
All inputs are finite; a program needn't handle non-finite values.
Results may differ from the reference program's by a relative error of at most 0.024.
The reference program's roundings to bfloat16 on the way count: a program that leaves them out, or rounds other values in their place, can miss the bound.
Values may be sent and summed in bfloat16 or wider, within the bound.
No kernel may reach another device: no remote copies, remote signals or barrier semaphores. Data moves between devices by JAX's collectives and lax.ppermute only.
A program may use at most 128 MiB of HBM per device.

```python
import jax
import jax.numpy as jnp
from jax import lax

D = 4096
HID = 1024
BLK = 128
WORDS = 8
FAN = 8
NB_DEV = 16
SEED_BLOCKS = 32
SEEDS = 4096
NODES = 65536
LISTS = 1024
N_NODE = 32


def draw_patterns(key, part):
    key_first, key_second = jax.random.split(key)
    pattern_shape = (LISTS, FAN, BLK, WORDS)
    first_bits = jax.random.randint(key_first, pattern_shape, 0, 65536, dtype=jnp.int32)
    second_bits = jax.random.randint(key_second, pattern_shape, 0, 65536, dtype=jnp.int32)
    packed = jnp.bitwise_and(first_bits, second_bits)
    return packed.at[0, 0, 0, 0].set(65535)


def draw_counts(key, part):
    groups = LISTS // SEED_BLOCKS
    key_level, key_place = jax.random.split(key)
    group_rank = jnp.arange(groups, dtype=jnp.int32)[:, None]
    count_level = 2 + (FAN - 2) * group_rank // max(groups - 1, 1)
    random_bits = jax.random.randint(key_level, (groups, SEED_BLOCKS), 0, 1048576, dtype=jnp.int32)
    drawn = 1 + random_bits % count_level
    forced_at = jax.random.randint(key_place, (), 0, SEED_BLOCKS, dtype=jnp.int32)
    drawn = drawn.at[groups - 1, forced_at].set(FAN)
    return drawn.reshape(LISTS).astype(jnp.int32)


def place_ends(values, own_key, smallest, high):
    dims = values.shape
    place = [jax.random.randint(jax.random.fold_in(own_key, axis), (), 0, dims[axis]) for axis in range(len(dims))]
    values = values.at[tuple(place)].set(smallest)
    longest = dims.index(max(dims))
    place[longest] = (place[longest] + 1) % dims[longest]
    return values.at[tuple(place)].set(high)


def with_spikes(entries, stream_key, source, target, shards_of, factor):
    owner, partner = [(jnp.arange(entries.shape[dim]) // (entries.shape[dim] // shards_of)).reshape([-1 if axis == dim else 1 for axis in range(entries.ndim)]) for dim in (source, target)]
    chosen = jax.random.permutation(stream_key, shards_of)[partner]
    strong = (owner == chosen) | (owner == (partner + shards_of // 2) % shards_of)
    return jnp.where(strong, factor * entries, entries)


def shard_levels(key, dims, cuts, smallest, largest):
    level = 1.0
    for dim, blocks in cuts:
        draws = jax.random.uniform(jax.random.fold_in(jax.random.fold_in(key, 6), dim), (blocks,), jnp.float32, smallest / len(cuts), largest / len(cuts))
        level = level * jnp.repeat(jnp.exp(draws), dims[dim] // blocks).reshape((-1,) + (1,) * (len(dims) - 1 - dim))
    return level


def bell_draw(own_key, shape, width, reach, pieces=(), kind=jnp.bfloat16):
    values = jax.random.normal(own_key, shape, jnp.float32) * width
    if len(pieces) > 0:
        values = shard_levels(own_key, shape, pieces, -0.22, 0.18) * values
    return jnp.clip(values, min=-reach, max=reach).astype(kind)


def heavy_noise(stream_key, extent, spread, bound, cuts, heavy, held_as=jnp.bfloat16):
    entries = spread * jax.random.normal(stream_key, extent, jnp.float32)
    if cuts:
        entries = entries * shard_levels(stream_key, extent, cuts, -0.22, 0.18)
    return jnp.clip(with_spikes(entries, jax.random.fold_in(stream_key, 3), *heavy), -bound, bound).astype(held_as)


def setup_inputs(seed: int = 0) -> dict:
    seeds = jax.random.split(jax.random.key(seed), 10)
    features = bell_draw(seeds[0], (NODES, D), 1.0, 6.0, ((0, 32), (1, 8)))
    seed_feats = heavy_noise(seeds[1], (SEEDS, D), 1.0, 6.0, ((0, 32), (1, 8)), (0, 1, 32, 2.75))
    patterns = draw_patterns(jax.random.fold_in(seeds[9], 71), 0)
    sources = place_ends(jax.random.randint(seeds[3], (LISTS, FAN), 0, NB_DEV), jax.random.fold_in(seeds[3], 1), 0, NB_DEV - 1).astype(jnp.int32)
    counts = draw_counts(jax.random.fold_in(seeds[9], 71), 0)
    w_self = bell_draw(seeds[5], (D, HID), D ** -0.5, 0.09375, ((0, 8),))
    w_neigh = bell_draw(seeds[6], (D, HID), D ** -0.5, 0.09375, ((0, 8),))
    bias_term = bell_draw(seeds[7], (HID,), 0.5, 3.0, (), jnp.float32)
    out_grad = bell_draw(seeds[8], (SEEDS, HID), ((SEEDS // 2) ** -0.5), 0.3125, ((0, 32),))
    return dict(features=features, seed_feats=seed_feats, patterns=patterns, sources=sources, counts=counts, w_self=w_self, w_neigh=w_neigh, bias_term=bias_term, out_grad=out_grad)


def unpack(packed):
    shifts = jnp.arange(16, dtype=jnp.int32)
    bit_values = jnp.bitwise_and(jnp.right_shift(packed[..., None], shifts), 1)
    return bit_values.reshape(packed.shape[:-1] + (packed.shape[-1] * 16,)).astype(jnp.float32)

def reference(features, seed_feats, patterns, sources, counts, w_self, w_neigh, bias_term, out_grad):
    feature_blocks = features.reshape(N_NODE, NB_DEV, BLK, D)
    pattern_rows = patterns.reshape(N_NODE, SEED_BLOCKS, FAN, BLK, WORDS)
    source_rows = sources.reshape(N_NODE, SEED_BLOCKS, FAN)
    count_rows = counts.reshape(N_NODE, SEED_BLOCKS)

    def one_source(state_pair, inputs):
        summed_rows, degree = state_pair
        block_feats, group_patterns, group_sources, group_counts = inputs
        live_mask = jnp.arange(FAN, dtype=jnp.int32)[None, :] < group_counts[:, None]
        for slot_index in range(FAN):
            tile_now = unpack(group_patterns[:, slot_index]) * live_mask[:, slot_index, None, None].astype(jnp.float32)
            chosen = block_feats[group_sources[:, slot_index]].astype(jnp.float32)
            summed_rows = summed_rows + jnp.einsum('trs,tsd->trd', tile_now, chosen)
            degree = degree + lax.optimization_barrier(jnp.sum(tile_now, axis=2))
        return ((summed_rows, degree), None)
    start_state = (jnp.zeros((SEED_BLOCKS, BLK, D), jnp.float32), jnp.zeros((SEED_BLOCKS, BLK), jnp.float32))
    (summed_rows, degree), _ = lax.scan(one_source, start_state, (feature_blocks, pattern_rows, source_rows, count_rows))
    aggregate = (summed_rows / jnp.sqrt(1.0 + degree)[:, :, None]).reshape(SEEDS, D).astype(jnp.bfloat16)
    pre_act = jnp.dot(seed_feats, w_self, preferred_element_type=jnp.float32)
    pre_act = pre_act + jnp.dot(aggregate, w_neigh, preferred_element_type=jnp.float32) + bias_term
    hidden = jnp.maximum(pre_act, 0.0).astype(jnp.bfloat16)
    grad_rows = jnp.where(pre_act > 0.0, out_grad, jnp.zeros_like(out_grad))
    grad_self = jnp.dot(seed_feats.T, grad_rows, preferred_element_type=jnp.float32)
    grad_neigh = jnp.dot(aggregate.T, grad_rows, preferred_element_type=jnp.float32)
    grad_bias = lax.optimization_barrier(jnp.sum(grad_rows.astype(jnp.float32), axis=0))
    return (hidden, grad_self, grad_neigh, grad_bias)
```

```python
import functools

import jax
import jax.numpy as jnp
from jax import lax
from jax.experimental import pallas as pl
from jax.experimental.pallas import tpu as pltpu
from jax.sharding import PartitionSpec as P

BLK = 128
HALF = 256
FAN = 8
TOP = 32700.0
NX, NZ, NY = 4, 4, 4
VMEM = pl.BlockSpec(memory_space=pltpu.VMEM)
SMEM = pl.BlockSpec(memory_space=pltpu.SMEM)
PARAMS = pltpu.CompilerParams(vmem_limit_bytes=48 * 1024 * 1024)


def node_of(x, z, c):
    return x * (NZ * 2) + z * 2 + c


def shift_x(d):
    return [
        (node_of(x, z, c), node_of((x + d) % NX, z, c))
        for x in range(NX) for z in range(NZ) for c in range(2)
    ]


def shift_z(d):
    return [
        (node_of(x, z, c), node_of(x, (z + d) % NZ, c))
        for x in range(NX) for z in range(NZ) for c in range(2)
    ]


SWAP_CORE = [(n, n ^ 1) for n in range(NX * NZ * 2)]
SWAP_FAR = [(f, f ^ 4) for f in range(8)]


def shift_y(d):
    return [(h * 4 + y, h * 4 + (y + d) % NY) for h in range(2) for y in range(NY)]


def split_kernel(core_ref, feat_ref, seed_ref, mine_ref, theirs_ref, smine_ref, stheirs_ref, turned, sturned):
    core = core_ref[0]
    turned[...] = feat_ref[...].T

    @pl.when(pl.program_id(0) == 0)
    def _():
        sturned[...] = seed_ref[...].T

    for block in range(16):
        keep = pl.ds(pl.multiple_of(block * 32 + core * 16, 16), 16)
        give = pl.ds(pl.multiple_of(block * 32 + (1 - core) * 16, 16), 16)
        rows = pl.ds(block * 16, 16)
        mine_ref[rows, :] = turned[keep, :]
        theirs_ref[rows, :] = turned[give, :]

        @pl.when(pl.program_id(0) == 0)
        def _():
            smine_ref[rows, :] = sturned[keep, :]
            stheirs_ref[rows, :] = sturned[give, :]


def split(core, features, seed_feats):
    nodes = features.shape[0]
    step = 512
    half = jax.ShapeDtypeStruct((HALF, nodes), jnp.bfloat16)
    shalf = jax.ShapeDtypeStruct((HALF, BLK), jnp.bfloat16)
    cols = pl.BlockSpec((HALF, step), lambda i, s: (0, i))
    whole = pl.BlockSpec((HALF, BLK), lambda i, s: (0, 0))
    return pl.pallas_call(
        split_kernel,
        out_shape=(half, half, shalf, shalf),
        grid_spec=pltpu.PrefetchScalarGridSpec(
            num_scalar_prefetch=1,
            grid=(nodes // step,),
            in_specs=[
                pl.BlockSpec((step, 512), lambda i, s: (i, 0)),
                pl.BlockSpec((BLK, 512), lambda i, s: (0, 0)),
            ],
            out_specs=[cols, cols, whole, whole],
            scratch_shapes=[pltpu.VMEM((512, step), jnp.bfloat16), pltpu.VMEM((512, BLK), jnp.bfloat16)],
        ),
        compiler_params=PARAMS,
        name="split",
    )(core, features, seed_feats)


def step_of(mantissa, exponent):
    return mantissa * jnp.exp2(exponent)


def encode(sums, count):
    top = jnp.maximum(jnp.max(jnp.abs(sums), axis=0, keepdims=True), 1e-25) * (1.0 / TOP)
    exponent = jnp.floor(jnp.log2(top)) - 13.0
    mantissa = jnp.ceil(top * jnp.exp2(-exponent))
    coded = jnp.round(sums * (1.0 / step_of(mantissa, exponent))).astype(jnp.int32).astype(jnp.int16)
    row = lax.broadcasted_iota(jnp.int32, (16, BLK), 0)
    tail = jnp.where(row == 0, count, jnp.where(row == 1, exponent, jnp.where(row == 2, mantissa, 0.0)))
    return coded, tail.astype(jnp.int32).astype(jnp.int16)


def decode(ref, index):
    tail = ref[index, pl.ds(HALF, 16), :].astype(jnp.int32).astype(jnp.float32)
    values = ref[index, pl.ds(0, HALF), :].astype(jnp.int32).astype(jnp.float32)
    return values * step_of(tail[2:3], tail[1:2]), tail[0:1]


def sums_kernel(coded_out, meta_ref, pat0_ref, pat1_ref, feat0_ref, feat1_ref, out_ref, acc, pop):
    target = meta_ref[0] + pl.program_id(0)
    shifts = lax.broadcasted_iota(jnp.int32, (FAN, 16, BLK), 1)
    acc[...] = jnp.zeros_like(acc)
    pop[...] = jnp.zeros_like(pop)
    for side, (pat_ref, feat_ref) in enumerate(((pat0_ref, feat0_ref), (pat1_ref, feat1_ref))):
        live = meta_ref[1 + side * 32 + target]

        def group(first):
            tiles, picked = [], []
            for slot in range(first, first + 4):
                words = pat_ref[0, slot] * (slot < live).astype(jnp.int32)
                pop[...] += lax.population_count(words)
                bits = (jnp.broadcast_to(words[:, None, :], (FAN, 16, BLK)) >> shifts) & 1
                tiles.append(bits.reshape(BLK, BLK).astype(jnp.float32).astype(jnp.bfloat16))
                source = meta_ref[65 + (side * 32 + target) * FAN + slot]
                picked.append(feat_ref[:, pl.ds(pl.multiple_of(source * BLK, BLK), BLK)])
            acc[...] += jnp.dot(
                jnp.concatenate(picked, axis=1), jnp.concatenate(tiles, axis=0),
                preferred_element_type=jnp.float32,
            )

        group(0)
        pl.when(live > 4)(functools.partial(group, 4))
    count = jnp.sum(pop[...], axis=0, keepdims=True).astype(jnp.float32)
    if coded_out:
        coded, tail = encode(acc[...], count)
        out_ref[0, pl.ds(0, HALF), :] = coded
        out_ref[0, pl.ds(HALF, 16), :] = tail
    else:
        out_ref[0, pl.ds(0, HALF), :] = acc[...]
        out_ref[0, pl.ds(HALF, 8), :] = jnp.broadcast_to(count, (8, BLK))


def sums(coded_out, meta, pat0, pat1, feat0, feat1):
    nodes = feat0.shape[1]
    pats = pl.BlockSpec((1, FAN, 8, BLK), lambda i, m: (m[0] + i, 0, 0, 0))
    feats = pl.BlockSpec((HALF, nodes), lambda i, m: (0, 0))
    rows, kind = (HALF + 16, jnp.int16) if coded_out else (HALF + 8, jnp.float32)
    return pl.pallas_call(
        functools.partial(sums_kernel, coded_out),
        out_shape=jax.ShapeDtypeStruct((8, rows, BLK), kind),
        grid_spec=pltpu.PrefetchScalarGridSpec(
            num_scalar_prefetch=1,
            grid=(8,),
            in_specs=[pats, pats, feats, feats],
            out_specs=pl.BlockSpec((1, rows, BLK), lambda i, m: (i, 0, 0)),
            scratch_shapes=[pltpu.VMEM((HALF, BLK), jnp.float32), pltpu.VMEM((8, BLK), jnp.int32)],
        ),
        compiler_params=PARAMS,
        cost_estimate=pl.CostEstimate(flops=2_000_000_000, bytes_accessed=3_000_000, transcendentals=0),
        name="sums",
    )(meta, pat0, pat1, feat0, feat1)


def merge_x_kernel(pos_ref, r1_ref, r2_ref, r3_ref, own_ref, kept_ref, o1_ref, o2_ref, o3_ref):
    z = pos_ref[1]
    for d, out_ref in enumerate((kept_ref, o1_ref, o2_ref, o3_ref)):
        for c in range(2):
            index = lax.rem(z + d, NZ) * 2 + c
            total = own_ref[index, pl.ds(0, HALF), :]
            count = own_ref[index, pl.ds(HALF, 8), :][0:1]
            for ref in (r1_ref, r2_ref, r3_ref):
                values, more = decode(ref, index)
                total += values
                count += more
            if d == 0:
                out_ref[c, pl.ds(0, HALF), :] = total
                out_ref[c, pl.ds(HALF, 8), :] = jnp.broadcast_to(count, (8, BLK))
            else:
                coded, tail = encode(total, count)
                out_ref[c, pl.ds(0, HALF), :] = coded
                out_ref[c, pl.ds(HALF, 16), :] = tail


def merge_x(pos, received, own):
    coded = jax.ShapeDtypeStruct((2, HALF + 16, BLK), jnp.int16)
    return pl.pallas_call(
        merge_x_kernel,
        out_shape=(jax.ShapeDtypeStruct((2, HALF + 8, BLK), jnp.float32), coded, coded, coded),
        in_specs=[SMEM] + [VMEM] * 4,
        out_specs=[VMEM] * 4,
        compiler_params=PARAMS,
        name="merge_x",
    )(pos, *received, own)


def merge_z_kernel(pos_ref, r1_ref, r2_ref, r3_ref, own_ref, mine_ref, theirs_ref):
    core = pos_ref[2]
    for out_ref, index in ((mine_ref, core), (theirs_ref, 1 - core)):
        total = own_ref[index, pl.ds(0, HALF), :]
        count = own_ref[index, pl.ds(HALF, 8), :][0:1]
        for ref in (r1_ref, r2_ref, r3_ref):
            values, more = decode(ref, index)
            total += values
            count += more
        out_ref[...] = (total / jnp.sqrt(1.0 + count)).astype(jnp.bfloat16)


def merge_z(pos, received, own):
    half = jax.ShapeDtypeStruct((HALF, BLK), jnp.bfloat16)
    return pl.pallas_call(
        merge_z_kernel,
        out_shape=(half, half),
        in_specs=[SMEM] + [VMEM] * 4,
        out_specs=[VMEM] * 2,
        compiler_params=PARAMS,
        name="merge_z",
    )(pos, *received, own)


def pre_kernel(pos_ref, mine_ref, other_ref, w_mine_ref, w_other_ref, self_ref, own_ref, o1_ref, o2_ref, o3_ref, acc):
    y = pos_ref[3]
    contract = (((0,), (0,)), ((), ()))
    acc[...] = (
        self_ref[...]
        + lax.dot_general(mine_ref[...], w_mine_ref[...], contract, preferred_element_type=jnp.float32)
        + lax.dot_general(other_ref[...], w_other_ref[...], contract, preferred_element_type=jnp.float32)
    )
    for d, out_ref in enumerate((own_ref, o1_ref, o2_ref, o3_ref)):
        out_ref[...] = acc[pl.ds(pl.multiple_of(lax.rem(y + d, NY) * 32, 32), 32), :]


def pre_terms(pos, mine, other, w_mine, w_other, self_term):
    hid = w_mine.shape[1]
    part = jax.ShapeDtypeStruct((BLK // NY, hid), jnp.float32)
    return pl.pallas_call(
        pre_kernel,
        out_shape=(part,) * 4,
        in_specs=[SMEM] + [VMEM] * 5,
        out_specs=[VMEM] * 4,
        scratch_shapes=[pltpu.VMEM((BLK, hid), jnp.float32)],
        compiler_params=PARAMS,
        name="pre_terms",
    )(pos, mine, other, w_mine, w_other, self_term)


def gather_kernel(pos_ref, own_ref, r1_ref, r2_ref, r3_ref, out_ref):
    y = pos_ref[3]
    for d, ref in enumerate((own_ref, r1_ref, r2_ref, r3_ref)):
        out_ref[pl.ds(pl.multiple_of(lax.rem(y + NY - d, NY) * 32, 32), 32), :] = ref[...]


def gather_hidden(pos, own, received):
    hid = own.shape[1]
    return pl.pallas_call(
        gather_kernel,
        out_shape=jax.ShapeDtypeStruct((BLK, hid), jnp.bfloat16),
        in_specs=[SMEM] + [VMEM] * 4,
        out_specs=VMEM,
        compiler_params=PARAMS,
        name="gather_hidden",
    )(pos, own, *received)


def grads_kernel(
    pos_ref, hid0_ref, hid1_ref, og0_ref, og1_ref, agg0_ref, agg1_ref, seed0_ref, seed1_ref,
    own_ref, o1_ref, o2_ref, o3_ref, acc_self, acc_neigh, bias,
):
    x = pos_ref[0]
    hid = hid0_ref.shape[1]
    zero = jnp.zeros_like(og0_ref)
    rows0 = jnp.where(hid0_ref[...] > 0, og0_ref[...], zero)
    rows1 = jnp.where(hid1_ref[...] > 0, og1_ref[...], zero)
    dot = functools.partial(jnp.dot, preferred_element_type=jnp.float32)
    acc_self[...] = dot(seed0_ref[...], rows0) + dot(seed1_ref[...], rows1)
    acc_neigh[...] = dot(agg0_ref[...], rows0) + dot(agg1_ref[...], rows1)
    total = jnp.sum(rows0.astype(jnp.float32), axis=0, keepdims=True) + jnp.sum(
        rows1.astype(jnp.float32), axis=0, keepdims=True
    )
    for part in range(8):
        bias[pl.ds(part, 1), :] = total[:, part * BLK:(part + 1) * BLK]
    row = lax.broadcasted_iota(jnp.int32, (16, BLK), 0)
    for d, out_ref in enumerate((own_ref, o1_ref, o2_ref, o3_ref)):
        to = lax.rem(x + d, NX)
        rows = pl.ds(pl.multiple_of(to * 64, 64), 64)
        out_ref[pl.ds(0, 64), pl.ds(0, hid)] = acc_self[rows, :].astype(out_ref.dtype)
        out_ref[pl.ds(64, 64), pl.ds(0, hid)] = acc_neigh[rows, :].astype(out_ref.dtype)
        tail = jnp.where(row == 0, bias[pl.ds(to * 2, 1), :], jnp.where(row == 1, bias[pl.ds(to * 2 + 1, 1), :], 0.0))
        if d > 0:
            high = tail.astype(jnp.bfloat16).astype(jnp.float32)
            low = tail - high
            low = jnp.concatenate([jnp.zeros((2, BLK), jnp.float32), low[:14]], axis=0)
            tail = high + low
        out_ref[pl.ds(0, 16), pl.ds(hid, BLK)] = tail.astype(out_ref.dtype)
        out_ref[pl.ds(16, 112), pl.ds(hid, BLK)] = jnp.zeros((112, BLK), out_ref.dtype)


def grads(pos, hid0, hid1, og0, og1, agg0, agg1, seed0, seed1):
    hid = hid0.shape[1]
    part = jax.ShapeDtypeStruct((BLK, hid + BLK), jnp.bfloat16)
    own = jax.ShapeDtypeStruct((BLK, hid + BLK), jnp.float32)
    return pl.pallas_call(
        grads_kernel,
        out_shape=(own, part, part, part),
        in_specs=[SMEM] + [VMEM] * 8,
        out_specs=[VMEM] * 4,
        scratch_shapes=[
            pltpu.VMEM((HALF, hid), jnp.float32),
            pltpu.VMEM((HALF, hid), jnp.float32),
            pltpu.VMEM((8, BLK), jnp.float32),
        ],
        compiler_params=PARAMS,
        name="grads",
    )(pos, hid0, hid1, og0, og1, agg0, agg1, seed0, seed1)


def merge_gx_kernel(pos_ref, r1_ref, r2_ref, r3_ref, own_ref, kept_ref, o1_ref, o2_ref, o3_ref, total, bias):
    z = pos_ref[1]
    hid = own_ref.shape[1] - BLK
    body = own_ref[:, pl.ds(0, hid)]
    tail = own_ref[pl.ds(0, 16), pl.ds(hid, BLK)]
    for ref in (r1_ref, r2_ref, r3_ref):
        body += ref[:, pl.ds(0, hid)].astype(jnp.float32)
        tail += ref[pl.ds(0, 16), pl.ds(hid, BLK)].astype(jnp.float32)
    total[...] = body
    bias[...] = jnp.concatenate([tail[0:2] + tail[2:4], jnp.zeros((6, BLK), jnp.float32)], axis=0)
    row = lax.broadcasted_iota(jnp.int32, (16, BLK), 0)
    for d, out_ref in enumerate((kept_ref, o1_ref, o2_ref, o3_ref)):
        to = lax.rem(z + d, NZ)
        out_ref[pl.ds(0, 16), pl.ds(0, hid)] = total[pl.ds(pl.multiple_of(to * 16, 16), 16), :].astype(out_ref.dtype)
        out_ref[pl.ds(16, 16), pl.ds(0, hid)] = total[pl.ds(pl.multiple_of(64 + to * 16, 16), 16), :].astype(out_ref.dtype)
        line = bias[pl.ds(to // 2, 1), :]
        if d > 0:
            high = line.astype(jnp.bfloat16).astype(jnp.float32)
            mark = jnp.where(row == 0, high, jnp.where(row == 1, line - high, 0.0))
        else:
            mark = jnp.where(row == 0, line, 0.0)
        out_ref[pl.ds(0, 16), pl.ds(hid, BLK)] = mark.astype(out_ref.dtype)
        out_ref[pl.ds(16, 16), pl.ds(hid, BLK)] = jnp.zeros((16, BLK), out_ref.dtype)


def merge_gx(pos, received, own):
    width = own.shape[1]
    part = jax.ShapeDtypeStruct((32, width), jnp.bfloat16)
    return pl.pallas_call(
        merge_gx_kernel,
        out_shape=(jax.ShapeDtypeStruct((32, width), jnp.float32), part, part, part),
        in_specs=[SMEM] + [VMEM] * 4,
        out_specs=[VMEM] * 4,
        scratch_shapes=[pltpu.VMEM((BLK, width - BLK), jnp.float32), pltpu.VMEM((8, BLK), jnp.float32)],
        compiler_params=PARAMS,
        name="merge_gx",
    )(pos, *received, own)


def merge_gz_kernel(r1_ref, r2_ref, r3_ref, own_ref, self_ref, neigh_ref, bias_ref):
    hid = self_ref.shape[1]
    body = own_ref[:, pl.ds(0, hid)]
    tail = own_ref[pl.ds(0, 16), pl.ds(hid, BLK)]
    for ref in (r1_ref, r2_ref, r3_ref):
        body += ref[:, pl.ds(0, hid)].astype(jnp.float32)
        tail += ref[pl.ds(0, 16), pl.ds(hid, BLK)].astype(jnp.float32)
    self_ref[...] = body[:16]
    neigh_ref[...] = body[16:]
    bias_ref[...] = jnp.broadcast_to(tail[0:1] + tail[1:2], (8, BLK))


def merge_gz(received, own):
    hid = own.shape[1] - BLK
    part = jax.ShapeDtypeStruct((16, hid), jnp.float32)
    return pl.pallas_call(
        merge_gz_kernel,
        out_shape=(part, part, jax.ShapeDtypeStruct((8, BLK), jnp.float32)),
        in_specs=[VMEM] * 4,
        out_specs=[VMEM] * 3,
        compiler_params=PARAMS,
        name="merge_gz",
    )(*received, own)


def halves(weights, core):
    hid = weights.shape[1]
    cut = weights.reshape(16, 2, 16, hid)
    take = lambda c: lax.dynamic_index_in_dim(cut, c, 1, keepdims=False).reshape(HALF, hid)
    return take(core), take(1 - core)


def body(features, seed_feats, patterns, sources, counts, w_self, w_neigh, bias_term, out_grad):
    node = lax.axis_index("node")
    feat = lax.axis_index("feat")
    x, z, core = node // (NZ * 2), (node // 2) % NZ, node % 2
    y = feat % NY
    pos = jnp.stack([x, z, core, y]).astype(jnp.int32)
    swap = lambda value: lax.ppermute(value, "node", SWAP_CORE)

    packed = patterns.transpose(0, 1, 3, 2)
    table = jnp.concatenate([counts, sources.reshape(-1)])
    packed_other, table_other = swap(packed), swap(table)
    mine, theirs, seed_mine, seed_theirs = split(pos[2:3], features, seed_feats)
    other, seed_other = swap(theirs), swap(seed_theirs)
    out_grad_other = swap(out_grad)
    lists = counts.shape[0]
    table = jnp.concatenate([table[:lists], table_other[:lists], table[lists:], table_other[lists:]])

    received = []
    for d in (2, 1, 3):
        meta = jnp.concatenate([((x + d) % NX * 8)[None].astype(jnp.int32), table])
        coded = sums(True, meta, packed, packed_other, mine, other)
        received.append(lax.ppermute(coded, "node", shift_x(d)))
    meta = jnp.concatenate([(x * 8)[None].astype(jnp.int32), table])
    own = sums(False, meta, packed, packed_other, mine, other)
    self_term = jnp.dot(seed_feats, w_self, preferred_element_type=jnp.float32)
    w_mine, w_other = halves(w_neigh, core)

    own, *coded = merge_x(pos, received, own)
    received = [lax.ppermute(coded[d - 1], "node", shift_z(d)) for d in (2, 1, 3)]
    agg_mine, agg_theirs = merge_z(pos, received, own)
    agg_other = swap(agg_theirs)

    own, *parts = pre_terms(pos, agg_mine, agg_other, w_mine, w_other, self_term)
    received = [lax.ppermute(parts[d - 1], "feat", shift_y(d)) for d in (2, 1, 3)]
    part = own + received[0] + received[1] + received[2]
    pre = part + lax.ppermute(part, "feat", SWAP_FAR) + bias_term
    own = jnp.maximum(pre, 0.0).astype(jnp.bfloat16)
    received = [lax.ppermute(own, "feat", shift_y(d)) for d in (1, 2, 3)]
    hidden = gather_hidden(pos, own, received)
    hidden_other = swap(hidden)

    own, *parts = grads(
        pos, hidden, hidden_other, out_grad, out_grad_other, agg_mine, agg_theirs, seed_mine, seed_other
    )
    received = [lax.ppermute(parts[d - 1], "node", shift_x(d)) for d in (2, 1, 3)]
    own, *parts = merge_gx(pos, received, own)
    received = [lax.ppermute(parts[d - 1], "node", shift_z(d)) for d in (2, 1, 3)]
    grad_self, grad_neigh, bias = merge_gz(received, own)
    grad_bias = lax.dynamic_slice(bias[0], (z % 2 * 64 + core * 32,), (32,))
    return (hidden, grad_self, grad_neigh, grad_bias)


def solution(mesh):
    return jax.shard_map(
        body,
        mesh=mesh,
        in_specs=(
            P("node", "feat"),
            P("node", "feat"),
            P("node", None, None, None),
            P("node", None),
            P("node"),
            P("feat", None),
            P("feat", None),
            P(),
            P("node", None),
        ),
        out_specs=(
            P("node", None),
            P(("feat", "node"), None),
            P(("feat", "node"), None),
            P("node"),
        ),
        check_vma=False,
    )
```

```python
import functools

import jax
import jax.numpy as jnp
from jax import lax
from jax.experimental import pallas as pl
from jax.experimental.pallas import tpu as pltpu
from jax.sharding import PartitionSpec as P

BLK = 128
HALF = 256
FAN = 8
TOP = 32700.0
NX, NZ, NY = 4, 4, 4
CUT = 640
VMEM = pl.BlockSpec(memory_space=pltpu.VMEM)
SMEM = pl.BlockSpec(memory_space=pltpu.SMEM)
PARAMS = pltpu.CompilerParams(vmem_limit_bytes=40 * 1024 * 1024)
F32 = functools.partial(lax.dot_general, preferred_element_type=jnp.float32)


def node_of(x, z, c):
    return x * (NZ * 2) + z * 2 + c


NODES = [(x, z, c) for x in range(NX) for z in range(NZ) for c in range(2)]
SWAP_CORE = [(n, n ^ 1) for n in range(NX * NZ * 2)]
SWAP_FAR = [(f, f ^ 4) for f in range(8)]


def shift_x(d):
    return [(node_of(x, z, c), node_of((x + d) % NX, z, c)) for x, z, c in NODES]


def shift_z(d):
    return [(node_of(x, z, c), node_of(x, (z + d) % NZ, c)) for x, z, c in NODES]


def shift_y(d):
    return [(h * 4 + y, h * 4 + (y + d) % NY) for h in range(2) for y in range(NY)]


def spread_x(j):
    return [(node_of(x, z, c), node_of(2 * c + (x + j) % 4 // 2, z, (x + j) % 2)) for x, z, c in NODES]


def step_of(mantissa, exponent):
    return mantissa * jnp.exp2(exponent)


def encode(sums, count):
    top = jnp.maximum(jnp.max(jnp.abs(sums), axis=0, keepdims=True), 1e-25) * (1.0 / TOP)
    exponent = jnp.floor(jnp.log2(top)) - 13.0
    mantissa = jnp.ceil(top * jnp.exp2(-exponent))
    coded = jnp.round(sums * (1.0 / step_of(mantissa, exponent))).astype(jnp.int32).astype(jnp.int16)
    row = lax.broadcasted_iota(jnp.int32, (16, BLK), 0)
    tail = jnp.where(row == 0, count, jnp.where(row == 1, exponent, jnp.where(row == 2, mantissa, 0.0)))
    return coded, tail.astype(jnp.int32).astype(jnp.int16)


def put_coded(ref, sums, count):
    coded, tail = encode(sums, count)
    ref[pl.ds(0, HALF), :] = coded
    ref[pl.ds(HALF, 16), :] = tail


def put_plain(ref, sums, count):
    ref[pl.ds(0, HALF), :] = sums
    ref[pl.ds(HALF, 8), :] = jnp.broadcast_to(count, (8, BLK))


def decode(ref):
    tail = ref[pl.ds(HALF, 16), :].astype(jnp.int32).astype(jnp.float32)
    values = ref[pl.ds(0, HALF), :].astype(jnp.int32).astype(jnp.float32)
    return values * step_of(tail[2:3], tail[1:2]), tail[0:1]


def gathered(own_ref, refs):
    total = own_ref[pl.ds(0, HALF), :]
    count = own_ref[pl.ds(HALF, 8), :][0:1]
    for ref in refs:
        values, more = decode(ref)
        total += values
        count += more
    return total, count


def sums_kernel(coded_out, meta_ref, pat0_ref, pat1_ref, feat0_ref, feat1_ref, even_ref, odd_ref, *scratch):
    tiles, accs, pops = scratch[0:2], scratch[2:4], scratch[4:7]
    pats, feats = (pat0_ref, pat1_ref), (feat0_ref, feat1_ref)
    blocks = pat0_ref.shape[0]
    slots = [(side, slot) for side in range(2) for slot in range(FAN)]
    put = put_coded if coded_out else put_plain

    def unpack(i, tile_ref, pop_ref):
        shifts = lax.broadcasted_iota(jnp.int32, (8, 16, BLK), 1)
        total = jnp.zeros((8, BLK), jnp.int32)
        for j, (side, slot) in enumerate(slots):
            live = meta_ref[2 + side * 32 + meta_ref[0] * blocks + i]
            words = pats[side][i, slot] * (slot < live).astype(jnp.int32)
            total += lax.population_count(words)
            bits = (jnp.broadcast_to(words[:, None, :], (8, 16, BLK)) >> shifts) & 1
            tile_ref[pl.ds(j * BLK, BLK), :] = bits.reshape(BLK, BLK).astype(jnp.float32).astype(jnp.bfloat16)
        pop_ref[...] = total

    def multiply(i, tile_ref, acc_ref):
        picked = []
        for side, slot in slots:
            source = meta_ref[66 + (side * 32 + meta_ref[0] * blocks + i) * FAN + slot]
            picked.append(feats[side][pl.ds(pl.multiple_of(source * BLK, BLK), BLK), :])
        acc_ref[...] = F32(tile_ref[...], jnp.concatenate(picked, axis=0), (((0,), (0,)), ((), ()))).T

    def finish(i, acc_ref, pop_ref):
        count = jnp.sum(pop_ref[...], axis=0, keepdims=True).astype(jnp.float32)
        put((even_ref, odd_ref)[i % 2].at[i // 2], acc_ref[...], count)

    for step in range(blocks + 2):
        if step < blocks:
            unpack(step, tiles[step % 2], pops[step % 3])
        if 0 <= step - 1 < blocks:
            multiply(step - 1, tiles[(step - 1) % 2], accs[(step - 1) % 2])
        if 0 <= step - 2 < blocks:
            finish(step - 2, accs[(step - 2) % 2], pops[(step - 2) % 3])


def sums(coded_out, meta, pat0, pat1, feat0, feat1):
    nodes = feat0.shape[0]
    blocks = 2 * NZ
    pats = pl.BlockSpec((blocks, FAN, 8, BLK), lambda i, m: (m[0], 0, 0, 0))
    rows, kind = (HALF + 16, jnp.int16) if coded_out else (HALF + 8, jnp.float32)
    part = pl.BlockSpec((NZ, rows, BLK), lambda i, m: (0, 0, 0))
    return pl.pallas_call(
        functools.partial(sums_kernel, coded_out),
        out_shape=[jax.ShapeDtypeStruct((NZ, rows, BLK), kind)] * 2,
        grid_spec=pltpu.PrefetchScalarGridSpec(
            num_scalar_prefetch=1,
            grid=(1,),
            in_specs=[
                pats,
                pats,
                pl.BlockSpec((nodes, HALF), lambda i, m: (0, m[1])),
                pl.BlockSpec((nodes, HALF), lambda i, m: (0, 0)),
            ],
            out_specs=[part, part],
            scratch_shapes=[pltpu.VMEM((2 * FAN * BLK, BLK), jnp.bfloat16)] * 2
            + [pltpu.VMEM((HALF, BLK), jnp.float32)] * 2
            + [pltpu.VMEM((8, BLK), jnp.int32)] * 3,
        ),
        compiler_params=PARAMS,
        cost_estimate=pl.CostEstimate(flops=2_000_000_000, bytes_accessed=3_000_000, transcendentals=0),
        name="sums",
    )(meta, pat0, pat1, feat0, feat1)


def merge_x_kernel(pos_ref, r1_ref, r2_ref, r3_ref, own_ref, kept_ref, o1_ref, o2_ref, o3_ref):
    for d, out_ref in enumerate((kept_ref, o1_ref, o2_ref, o3_ref)):
        index = lax.rem(pos_ref[1] + d, NZ)
        total, count = gathered(own_ref.at[index], [ref.at[index] for ref in (r1_ref, r2_ref, r3_ref)])
        (put_coded if d else put_plain)(out_ref, total, count)


def call(kernel, name, outs, count, scratch=()):
    return pl.pallas_call(
        kernel,
        out_shape=outs,
        in_specs=[SMEM] + [VMEM] * count,
        out_specs=[VMEM] * len(outs),
        scratch_shapes=list(scratch),
        compiler_params=PARAMS,
        name=name,
    )


def shaped(rows, cols, kind):
    return jax.ShapeDtypeStruct((rows, cols), kind)


CODED = shaped(HALF + 16, BLK, jnp.int16)
PLAIN = shaped(HALF + 8, BLK, jnp.float32)
HALF16 = shaped(HALF, BLK, jnp.bfloat16)


def merge_x(pos, received, own):
    return call(merge_x_kernel, "merge_x", [PLAIN] + [CODED] * 3, 4)(pos, *received, own)


def merge_z_kernel(pos_ref, a1_ref, a2_ref, a3_ref, a_ref, b1_ref, b2_ref, b3_ref, b_ref, mine_ref, theirs_ref):
    both = []
    for own_ref, refs in ((a_ref, (a1_ref, a2_ref, a3_ref)), (b_ref, (b1_ref, b2_ref, b3_ref))):
        total, count = gathered(own_ref, refs)
        both.append(total / jnp.sqrt(1.0 + count))
    first = pos_ref[2] == 0
    mine_ref[...] = jnp.where(first, both[0], both[1]).astype(jnp.bfloat16)
    theirs_ref[...] = jnp.where(first, both[1], both[0]).astype(jnp.bfloat16)


def pre_kernel(pos_ref, mine_ref, other_ref, w_ref, self_ref, own_ref, o1_ref, o2_ref, o3_ref):
    core, y = pos_ref[2], pos_ref[3]
    mine = pl.ds(pl.multiple_of(core * HALF, HALF), HALF)
    other = pl.ds(pl.multiple_of((1 - core) * HALF, HALF), HALF)
    contract = (((1,), (0,)), ((), ()))
    for d, out_ref in enumerate((own_ref, o1_ref, o2_ref, o3_ref)):
        rows = pl.ds(pl.multiple_of(lax.rem(y + d, NY) * HALF, HALF), HALF)
        terms = self_ref[rows, :] + F32(w_ref[rows, mine], mine_ref[...], contract)
        terms += F32(w_ref[rows, other], other_ref[...], contract)
        if d:
            put_coded(out_ref, terms, 0.0)
        else:
            put_plain(out_ref, terms, jnp.zeros((1, BLK), jnp.float32))


def merge_y_kernel(pos_ref, r1_ref, r2_ref, r3_ref, own_ref, out_ref):
    total, _ = gathered(own_ref, (r1_ref, r2_ref, r3_ref))
    put_coded(out_ref, total, 0.0)


def hidden_kernel(pos_ref, own_ref, far_ref, bias_ref, out_ref):
    pre = decode(own_ref)[0] + decode(far_ref)[0] + bias_ref[...]
    out_ref[...] = jnp.maximum(pre, 0.0).astype(jnp.bfloat16)


def grads_kernel(
    pos_ref, a0_ref, a1_ref, a2_ref, a3_ref, b0_ref, b1_ref, b2_ref, b3_ref, og0_ref, og1_ref,
    agg0_ref, agg1_ref, seed0_ref, seed1_ref,
    hidden_ref, j0_ref, j1_ref, j2_ref, j3_ref, kept_ref, d1_ref, d2_ref, d3_ref,
    turned, rows, self_acc, neigh_acc, bias,
):
    x, z, y = pos_ref[0], pos_ref[1], pos_ref[3]
    zero = jnp.zeros((HALF, BLK), jnp.bfloat16)
    for d in range(NY):
        place = pl.ds(pl.multiple_of(lax.rem(y + NY - d, NY) * HALF, HALF), HALF)
        for side, (refs, og_ref) in enumerate(
            (((a0_ref, a1_ref, a2_ref, a3_ref), og0_ref), ((b0_ref, b1_ref, b2_ref, b3_ref), og1_ref))
        ):
            value = refs[d][...]
            if side == 0:
                turned[place, :] = value
            rows[place, pl.ds(side * BLK, BLK)] = jnp.where(value > 0, og_ref[place, :], zero)
    hid = rows.shape[0]
    contract = (((1,), (1,)), ((), ()))
    seeds = jnp.concatenate([seed0_ref[...], seed1_ref[...]], axis=1)
    aggs = jnp.concatenate([agg0_ref[...], agg1_ref[...]], axis=1)
    self_acc[...] = F32(seeds, rows[...], contract)
    neigh_acc[...] = F32(aggs, rows[...], contract)
    total = F32(jnp.ones((8, 2 * BLK), jnp.bfloat16), rows[...], contract)[0:1]
    for part in range(hid // BLK):
        bias[pl.ds(part, 1), :] = total[:, part * BLK:(part + 1) * BLK]
    row = lax.broadcasted_iota(jnp.int32, (16, BLK), 0)
    first, second = pl.ds(0, CUT), pl.ds(CUT, hid - CUT)
    for j, out_ref in enumerate((j0_ref, j1_ref, j2_ref, j3_ref)):
        turn = lax.rem(x + j, 4)
        a, b = turn // 2, lax.rem(turn, 2)
        for to in range(NZ):
            take = pl.ds(pl.multiple_of(a * 128 + to * 32 + b * 16, 16), 16)
            out_ref[pl.ds(to * 16, 16), first] = self_acc[take, first].astype(jnp.bfloat16)
            out_ref[pl.ds(64 + to * 16, 16), first] = neigh_acc[take, first].astype(jnp.bfloat16)
        line = (2 * pos_ref[2] + a) * 2
        low_line = bias[pl.ds(line, 1), :]
        high_line = bias[pl.ds(line + 1, 1), :]
        low_top = low_line.astype(jnp.bfloat16).astype(jnp.float32)
        high_top = high_line.astype(jnp.bfloat16).astype(jnp.float32)
        mark = jnp.where(row == 0, low_top, jnp.where(row == 1, high_top, 0.0))
        mark = jnp.where(row == 2, low_line - low_top, jnp.where(row == 3, high_line - high_top, mark))
        out_ref[pl.ds(0, 16), pl.ds(CUT, BLK)] = mark.astype(jnp.bfloat16)
        out_ref[pl.ds(16, 112), pl.ds(CUT, BLK)] = jnp.zeros((112, BLK), jnp.bfloat16)
    for d, out_ref in enumerate((kept_ref, d1_ref, d2_ref, d3_ref)):
        to = lax.rem(z + d, NZ)
        for a in range(2):
            take = pl.ds(pl.multiple_of(a * 128 + to * 32, 32), 32)
            out_ref[pl.ds(a * 32, 32), :] = self_acc[take, second].astype(out_ref.dtype)
            out_ref[pl.ds(64 + a * 32, 32), :] = neigh_acc[take, second].astype(out_ref.dtype)
    for part in range(hid // BLK):
        cols = pl.ds(part * BLK, BLK)
        hidden_ref[:, cols] = turned[cols, :].T


def grads(pos, hid):
    outs = [shaped(BLK, hid, jnp.bfloat16)] + [shaped(BLK, CUT + BLK, jnp.bfloat16)] * 4
    outs += [shaped(BLK, hid - CUT, jnp.float32)] + [shaped(BLK, hid - CUT, jnp.bfloat16)] * 3
    scratch = [
        pltpu.VMEM((hid, BLK), jnp.bfloat16),
        pltpu.VMEM((hid, 2 * BLK), jnp.bfloat16),
        pltpu.VMEM((HALF, hid), jnp.float32),
        pltpu.VMEM((HALF, hid), jnp.float32),
        pltpu.VMEM((8, BLK), jnp.float32),
    ]
    return functools.partial(call(grads_kernel, "grads", outs, 14, scratch), pos)


def fold_x_kernel(pos_ref, r0_ref, r1_ref, r2_ref, r3_ref, kept_ref, d1_ref, d2_ref, d3_ref, total, bias):
    body, marks = pl.ds(0, CUT), pl.ds(CUT, BLK)
    refs = (r0_ref, r1_ref, r2_ref, r3_ref)
    total[...] = sum(ref[:, body].astype(jnp.float32) for ref in refs)
    mark = sum(ref[pl.ds(0, 16), marks].astype(jnp.float32) for ref in refs)
    bias[pl.ds(0, 1), :] = mark[0:1] + mark[2:3]
    bias[pl.ds(1, 1), :] = mark[1:2] + mark[3:4]
    row = lax.broadcasted_iota(jnp.int32, (16, BLK), 0)
    for d, out_ref in enumerate((kept_ref, d1_ref, d2_ref, d3_ref)):
        to = lax.rem(pos_ref[1] + d, NZ)
        for kind in range(2):
            take = pl.ds(pl.multiple_of(kind * 64 + to * 16, 16), 16)
            out_ref[pl.ds(kind * 16, 16), body] = total[take, :].astype(out_ref.dtype)
        line = bias[pl.ds(to // 2, 1), :]
        top = line.astype(jnp.bfloat16).astype(jnp.float32) if d else line
        mark = jnp.where(row == 0, top, jnp.where(row == 1, line - top, 0.0))
        out_ref[pl.ds(0, 16), marks] = mark.astype(out_ref.dtype)
        out_ref[pl.ds(16, 16), marks] = jnp.zeros((16, BLK), out_ref.dtype)


def fold_z_kernel(pos_ref, r1_ref, r2_ref, r3_ref, own_ref, j0_ref, j1_ref, j2_ref, j3_ref, total):
    total[...] = own_ref[...] + sum(ref[...].astype(jnp.float32) for ref in (r1_ref, r2_ref, r3_ref))
    for j, out_ref in enumerate((j0_ref, j1_ref, j2_ref, j3_ref)):
        turn = lax.rem(pos_ref[0] + j, 4)
        for kind in range(2):
            take = pl.ds(pl.multiple_of(kind * 64 + turn * 16, 16), 16)
            out_ref[pl.ds(kind * 16, 16), :] = total[take, :].astype(jnp.bfloat16)


def last_kernel(
    pos_ref, z1_ref, z2_ref, z3_ref, z0_ref, x0_ref, x1_ref, x2_ref, x3_ref, self_ref, neigh_ref, bias_ref
):
    hid = self_ref.shape[1]
    body, marks, rest = pl.ds(0, CUT), pl.ds(CUT, BLK), pl.ds(CUT, hid - CUT)
    left = z0_ref[:, body] + sum(ref[:, body].astype(jnp.float32) for ref in (z1_ref, z2_ref, z3_ref))
    right = sum(ref[...].astype(jnp.float32) for ref in (x0_ref, x1_ref, x2_ref, x3_ref))
    top = pl.ds(0, 16)
    mark = z0_ref[top, marks] + sum(ref[top, marks].astype(jnp.float32) for ref in (z1_ref, z2_ref, z3_ref))
    self_ref[:, body] = left[:16]
    self_ref[:, rest] = right[:16]
    neigh_ref[:, body] = left[16:]
    neigh_ref[:, rest] = right[16:]
    bias_ref[...] = jnp.broadcast_to(mark[0:1] + mark[1:2], (8, BLK))


def body(features, seed_feats, patterns, sources, counts, w_self, w_neigh, bias_term, out_grad):
    node = lax.axis_index("node")
    feat = lax.axis_index("feat")
    x, z, core = node // (NZ * 2), (node // 2) % NZ, node % 2
    y = feat % NY
    pos = jnp.stack([x, z, core, y]).astype(jnp.int32)
    hid = w_self.shape[1]
    swap = lambda value: lax.ppermute(value, "node", SWAP_CORE)

    packed = patterns.transpose(0, 1, 3, 2)
    table = jnp.concatenate([counts, sources.reshape(-1)])
    other = swap(lax.dynamic_slice_in_dim(features, (1 - core) * HALF, HALF, 1))
    packed_other, table_other = swap(packed), swap(table)
    lists = counts.shape[0]
    table = jnp.concatenate([table[:lists], table_other[:lists], table[lists:], table_other[lists:]])

    made = {}
    for d in (2, 1, 3, 0):
        meta = jnp.concatenate([jnp.stack([(x + d) % NX, core]).astype(jnp.int32), table])
        made[d] = sums(d > 0, meta, packed, packed_other, features, other)
    sent = [[lax.ppermute(made[d][part], "node", shift_x(d)) for d in (2, 1, 3)] for part in range(2)]

    seed_feats, w_self, w_neigh, bias_term, out_grad, made[0] = lax.optimization_barrier(
        (seed_feats, w_self, w_neigh, bias_term, out_grad, made[0])
    )
    seed_turned = seed_feats.T
    seed_mine = lax.dynamic_slice_in_dim(seed_turned, core * HALF, HALF, 0)
    seed_other = swap(lax.dynamic_slice_in_dim(seed_turned, (1 - core) * HALF, HALF, 0))
    og_turned = out_grad.T
    og_other = swap(og_turned)
    w_turned = w_neigh.T
    self_term = F32(w_self, seed_feats, (((0,), (1,)), ((), ())))
    bias_rows = jnp.broadcast_to(lax.dynamic_slice_in_dim(bias_term, y * HALF, HALF, 0)[:, None], (HALF, BLK))

    arrived = []
    for part in range(2):
        own, *coded = merge_x(pos, sent[part], made[0][part])
        arrived += [lax.ppermute(coded[d - 1], "node", shift_z(d)) for d in (2, 1, 3)] + [own]
    agg_mine, agg_theirs = call(merge_z_kernel, "merge_z", [HALF16] * 2, 8)(pos, *arrived)
    agg_other = swap(agg_theirs)

    own, *coded = call(pre_kernel, "pre_terms", [PLAIN] + [CODED] * 3, 4)(
        pos, agg_mine, agg_other, w_turned, self_term
    )
    received = [lax.ppermute(coded[d - 1], "feat", shift_y(d)) for d in (2, 1, 3)]
    (coded,) = call(merge_y_kernel, "merge_y", [CODED], 4)(pos, *received, own)
    far = lax.ppermute(coded, "feat", SWAP_FAR)
    (own,) = call(hidden_kernel, "hidden", [HALF16], 3)(pos, coded, far, bias_rows)
    chunks = [own] + [lax.ppermute(own, "feat", shift_y(d)) for d in (1, 2, 3)]
    chunks_other = [swap(chunk) for chunk in chunks]

    outs = grads(pos, hid)(
        *chunks, *chunks_other, og_turned, og_other, agg_mine, agg_theirs, seed_mine, seed_other
    )
    hidden, by_x, own, by_z = outs[0], outs[1:5], outs[5], outs[6:9]
    by_x = [lax.ppermute(by_x[j], "node", spread_x(j)) for j in range(4)]
    by_z = [lax.ppermute(by_z[d - 1], "node", shift_z(d)) for d in (2, 1, 3)]
    part = shaped(32, CUT + BLK, jnp.bfloat16)
    kept, *then_z = call(
        fold_x_kernel, "fold_x", [shaped(32, CUT + BLK, jnp.float32)] + [part] * 3, 4,
        [pltpu.VMEM((BLK, CUT), jnp.float32), pltpu.VMEM((8, BLK), jnp.float32)],
    )(pos, *by_x)
    then_z = [lax.ppermute(then_z[d - 1], "node", shift_z(d)) for d in (2, 1, 3)]
    then_x = call(
        fold_z_kernel, "fold_z", [shaped(32, hid - CUT, jnp.bfloat16)] * 4, 4,
        [pltpu.VMEM((BLK, hid - CUT), jnp.float32)],
    )(pos, *by_z, own)
    then_x = [lax.ppermute(then_x[j], "node", spread_x(j)) for j in range(4)]
    part = shaped(16, hid, jnp.float32)
    grad_self, grad_neigh, bias = call(last_kernel, "last", [part, part, shaped(8, BLK, jnp.float32)], 8)(
        pos, *then_z, kept, *then_x
    )
    grad_bias = lax.dynamic_slice(bias[0], (z % 2 * 64 + core * 32,), (32,))
    return (hidden, grad_self, grad_neigh, grad_bias)


def solution(mesh):
    return jax.shard_map(
        body,
        mesh=mesh,
        in_specs=(
            P("node", "feat"),
            P("node", "feat"),
            P("node", None, None, None),
            P("node", None),
            P("node"),
            P("feat", None),
            P("feat", None),
            P(),
            P("node", None),
        ),
        out_specs=(
            P("node", None),
            P(("feat", "node"), None),
            P(("feat", "node"), None),
            P("node"),
        ),
        check_vma=False,
    )
```

```python
import functools

import jax
import jax.numpy as jnp
from jax import lax
from jax.experimental import pallas as pl
from jax.experimental.pallas import tpu as pltpu
from jax.sharding import PartitionSpec as P

BLK = 128
HALF = 256
FAN = 8
TOP = 32700.0
NX, NZ, NY = 4, 4, 4
WIDE = 512
VMEM = pl.BlockSpec(memory_space=pltpu.VMEM)
SMEM = pl.BlockSpec(memory_space=pltpu.SMEM)
PARAMS = pltpu.CompilerParams(vmem_limit_bytes=40 * 1024 * 1024)
F32 = functools.partial(lax.dot_general, preferred_element_type=jnp.float32)


def node_of(x, z, c):
    return x * (NZ * 2) + z * 2 + c


NODES = [(x, z, c) for x in range(NX) for z in range(NZ) for c in range(2)]
SWAP_CORE = [(n, n ^ 1) for n in range(NX * NZ * 2)]
SWAP_FAR = [(f, f ^ 4) for f in range(8)]


def shift_x(d):
    return [(node_of(x, z, c), node_of((x + d) % NX, z, c)) for x, z, c in NODES]


def shift_z(d):
    return [(node_of(x, z, c), node_of(x, (z + d) % NZ, c)) for x, z, c in NODES]


def shift_y(d):
    return [(h * 4 + y, h * 4 + (y + d) % NY) for h in range(2) for y in range(NY)]


def step_of(mantissa, exponent):
    return mantissa * jnp.exp2(exponent)


def encode(sums, count):
    top = jnp.maximum(jnp.max(jnp.abs(sums), axis=0, keepdims=True), 1e-25) * (1.0 / TOP)
    exponent = jnp.floor(jnp.log2(top)) - 13.0
    mantissa = jnp.ceil(top * jnp.exp2(-exponent))
    coded = jnp.round(sums * (1.0 / step_of(mantissa, exponent))).astype(jnp.int32).astype(jnp.int16)
    row = lax.broadcasted_iota(jnp.int32, (16, BLK), 0)
    tail = jnp.where(row == 0, count, jnp.where(row == 1, exponent, jnp.where(row == 2, mantissa, 0.0)))
    return coded, tail.astype(jnp.int32).astype(jnp.int16)


def put_coded(ref, sums, count):
    rows = sums.shape[0]
    coded, tail = encode(sums, count)
    ref[pl.ds(0, rows), :] = coded
    ref[pl.ds(rows, 16), :] = tail


def put_plain(ref, sums, count):
    rows = sums.shape[0]
    ref[pl.ds(0, rows), :] = sums
    ref[pl.ds(rows, 8), :] = jnp.broadcast_to(count, (8, BLK))


def plain(ref):
    rows = ref.shape[0] - 8
    return ref[pl.ds(0, rows), :], ref[pl.ds(rows, 8), :][0:1]


def decode(ref):
    rows = ref.shape[0] - 16
    tail = ref[pl.ds(rows, 16), :].astype(jnp.int32).astype(jnp.float32)
    values = ref[pl.ds(0, rows), :].astype(jnp.int32).astype(jnp.float32)
    return values * step_of(tail[2:3], tail[1:2]), tail[0:1]


def gathered(plain_refs, coded_refs):
    pairs = [plain(ref) for ref in plain_refs] + [decode(ref) for ref in coded_refs]
    return sum(pair[0] for pair in pairs), sum(pair[1] for pair in pairs)


def sums_kernel(coded_out, meta_ref, pat0_ref, pat1_ref, feat0_ref, feat1_ref, out_ref, *scratch):
    tiles, accs, pops = scratch[0:2], scratch[2:4], scratch[4:7]
    pats, feats = (pat0_ref, pat1_ref), (feat0_ref, feat1_ref)
    blocks = pat0_ref.shape[0]
    slots = [(side, slot) for side in range(2) for slot in range(FAN)]
    put = put_coded if coded_out else put_plain

    def unpack(i, tile_ref, pop_ref):
        shifts = lax.broadcasted_iota(jnp.int32, (8, 16, BLK), 1)
        total = jnp.zeros((8, BLK), jnp.int32)
        for j, (side, slot) in enumerate(slots):
            live = meta_ref[2 + side * 32 + meta_ref[0] * blocks + i]
            words = pats[side][i, slot] * (slot < live).astype(jnp.int32)
            total += lax.population_count(words)
            bits = (jnp.broadcast_to(words[:, None, :], (8, 16, BLK)) >> shifts) & 1
            tile_ref[pl.ds(j * BLK, BLK), :] = bits.reshape(BLK, BLK).astype(jnp.float32).astype(jnp.bfloat16)
        pop_ref[...] = total

    def multiply(i, tile_ref, acc_ref):
        picked = []
        for side, slot in slots:
            source = meta_ref[66 + (side * 32 + meta_ref[0] * blocks + i) * FAN + slot]
            picked.append(feats[side][pl.ds(pl.multiple_of(source * BLK, BLK), BLK), :])
        acc_ref[...] = F32(tile_ref[...], jnp.concatenate(picked, axis=0), (((0,), (0,)), ((), ()))).T

    def finish(i, acc_ref, pop_ref):
        count = jnp.sum(pop_ref[...], axis=0, keepdims=True).astype(jnp.float32)
        put(out_ref.at[i], acc_ref[...], count)

    for step in range(blocks + 2):
        if step < blocks:
            unpack(step, tiles[step % 2], pops[step % 3])
        if 0 <= step - 1 < blocks:
            multiply(step - 1, tiles[(step - 1) % 2], accs[(step - 1) % 2])
        if 0 <= step - 2 < blocks:
            finish(step - 2, accs[(step - 2) % 2], pops[(step - 2) % 3])


def sums(coded_out, meta, pat0, pat1, feat0, feat1):
    blocks = 2 * NZ
    pats = pl.BlockSpec((blocks, FAN, 8, BLK), lambda i, m: (m[0], 0, 0, 0))
    rows, kind = (HALF + 16, jnp.int16) if coded_out else (HALF + 8, jnp.float32)
    return pl.pallas_call(
        functools.partial(sums_kernel, coded_out),
        out_shape=jax.ShapeDtypeStruct((blocks, rows, BLK), kind),
        grid_spec=pltpu.PrefetchScalarGridSpec(
            num_scalar_prefetch=1,
            grid=(1,),
            in_specs=[
                pats,
                pats,
                pl.BlockSpec((feat0.shape[0], HALF), lambda i, m: (0, m[1])),
                pl.BlockSpec(feat1.shape, lambda i, m: (0, 0)),
            ],
            out_specs=pl.BlockSpec((blocks, rows, BLK), lambda i, m: (0, 0, 0)),
            scratch_shapes=[pltpu.VMEM((2 * FAN * BLK, BLK), jnp.bfloat16)] * 2
            + [pltpu.VMEM((HALF, BLK), jnp.float32)] * 2
            + [pltpu.VMEM((8, BLK), jnp.int32)] * 3,
        ),
        compiler_params=PARAMS,
        cost_estimate=pl.CostEstimate(flops=2_000_000_000, bytes_accessed=3_000_000, transcendentals=0),
        name="sums",
    )(meta, pat0, pat1, feat0, feat1)


def call(kernel, name, outs, count, scratch=(), waits=0):
    return pl.pallas_call(
        kernel,
        out_shape=outs,
        in_specs=[SMEM] + [VMEM] * count + [pl.BlockSpec(memory_space=pl.ANY)] * waits,
        out_specs=[VMEM] * len(outs),
        scratch_shapes=list(scratch),
        compiler_params=PARAMS,
        name=name,
    )


def shaped(*dims):
    return jax.ShapeDtypeStruct(dims[:-1], dims[-1])


SUM_CODED = shaped(2, HALF + 16, BLK, jnp.int16)
SUM_PLAIN = shaped(2, HALF + 8, BLK, jnp.float32)
CODED = shaped(HALF + 16, BLK, jnp.int16)
PLAIN = shaped(HALF + 8, BLK, jnp.float32)
HALF16 = shaped(HALF, BLK, jnp.bfloat16)


def merge_x_kernel(pos_ref, r1_ref, r2_ref, r3_ref, own_ref, *rest):
    for d, out_ref in enumerate(rest[-4:]):
        for c in range(2):
            index = lax.rem(pos_ref[1] + d, NZ) * 2 + c
            total, count = gathered((own_ref.at[index],), [ref.at[index] for ref in (r1_ref, r2_ref, r3_ref)])
            (put_coded if d else put_plain)(out_ref.at[c], total, count)


def merge_z_kernel(pos_ref, r1_ref, r2_ref, r3_ref, own_ref, mine_ref, give_ref, rest_ref):
    core = pos_ref[2]
    for out_ref, index in ((mine_ref, core), (give_ref, 1 - core)):
        total, count = gathered((own_ref.at[index],), [ref.at[index] for ref in (r1_ref, r2_ref, r3_ref)])
        out_ref[pl.ds(0, HALF), :] = (total / jnp.sqrt(1.0 + count)).astype(jnp.bfloat16)
    for block in range(HALF // 32):
        keep = pl.ds(pl.multiple_of(block * 32 + core * 16, 16), 16)
        give = pl.ds(pl.multiple_of(block * 32 + 16 - core * 16, 16), 16)
        give_ref[pl.ds(HALF + block * 16, 16), :] = mine_ref[give, :]
        rest_ref[pl.ds(block * 16, 16), :] = give_ref[keep, :]


def pre_kernel(
    pos_ref, mine_ref, got_ref, rest_ref, w_ref, self_ref, own_ref, o1_ref, o2_ref, o3_ref, agg0_ref, agg1_ref, agg, acc
):
    core = pos_ref[2]
    agg[pl.ds(pl.multiple_of(core * HALF, HALF), HALF), :] = mine_ref[...]
    agg[pl.ds(pl.multiple_of((1 - core) * HALF, HALF), HALF), :] = got_ref[pl.ds(0, HALF), :]
    acc[...] = (self_ref[...] + F32(agg[...], w_ref[...], (((0,), (0,)), ((), ())))).T
    for d, out_ref in enumerate((own_ref, o1_ref, o2_ref, o3_ref)):
        terms = acc[pl.ds(pl.multiple_of(lax.rem(pos_ref[3] + d, NY) * HALF, HALF), HALF), :]
        (put_coded if d else put_plain)(out_ref, terms, jnp.zeros((1, BLK), jnp.float32))
    for block in range(WIDE // 32):
        rows = pl.ds(pl.multiple_of(block * 32 + core * 16, 16), 16)
        agg0_ref[pl.ds(block * 16, 16), :] = agg[rows, :]
    agg1_ref[pl.ds(pl.multiple_of(core * BLK, BLK), BLK), :] = rest_ref[...]
    agg1_ref[pl.ds(pl.multiple_of((1 - core) * BLK, BLK), BLK), :] = got_ref[pl.ds(HALF, BLK), :]


def merge_y_kernel(pos_ref, r1_ref, r2_ref, r3_ref, own_ref, out_ref):
    total, count = gathered((own_ref,), (r1_ref, r2_ref, r3_ref))
    put_coded(out_ref, total, count)


def hidden_kernel(pos_ref, own_ref, far_ref, out_ref):
    out_ref[...] = jnp.maximum(decode(own_ref)[0] + decode(far_ref)[0], 0.0).astype(jnp.bfloat16)


def grads_kernel(
    pos_ref, a0_ref, a1_ref, a2_ref, a3_ref, b0_ref, b1_ref, b2_ref, b3_ref, og0_ref, og1_ref,
    agg0_ref, agg1_ref, seed0_ref, seed1_ref,
    hidden_ref, own_ref, o1_ref, o2_ref, o3_ref, rows, self_acc, neigh_acc, bias,
):
    x, y = pos_ref[0], pos_ref[3]
    zero = jnp.zeros((BLK, HALF), jnp.bfloat16)
    for d in range(NY):
        place = pl.ds(pl.multiple_of(lax.rem(y + NY - d, NY) * HALF, HALF), HALF)
        for side, (refs, og_ref) in enumerate(
            (((a0_ref, a1_ref, a2_ref, a3_ref), og0_ref), ((b0_ref, b1_ref, b2_ref, b3_ref), og1_ref))
        ):
            value = refs[d][...].T
            if side == 0:
                hidden_ref[:, place] = value
            rows[pl.ds(side * BLK, BLK), place] = jnp.where(value > 0, og_ref[:, place], zero)
    hid = rows.shape[1]
    contract = (((1,), (0,)), ((), ()))
    self_acc[...] = F32(jnp.concatenate([seed0_ref[...], seed1_ref[...]], axis=1), rows[...], contract)
    neigh_acc[...] = F32(jnp.concatenate([agg0_ref[...], agg1_ref[...]], axis=1), rows[...], contract)
    total = F32(jnp.ones((8, 2 * BLK), jnp.bfloat16), rows[...], contract)[0:1]
    for part in range(hid // BLK):
        bias[pl.ds(part, 1), :] = total[:, part * BLK:(part + 1) * BLK]
    row = lax.broadcasted_iota(jnp.int32, (16, BLK), 0)
    for d, out_ref in enumerate((own_ref, o1_ref, o2_ref, o3_ref)):
        to = lax.rem(x + d, NX)
        take = pl.ds(pl.multiple_of(to * 64, 64), 64)
        out_ref[pl.ds(0, 64), pl.ds(0, hid)] = self_acc[take, :].astype(out_ref.dtype)
        out_ref[pl.ds(64, 64), pl.ds(0, hid)] = neigh_acc[take, :].astype(out_ref.dtype)
        left, right = bias[pl.ds(to * 2, 1), :], bias[pl.ds(to * 2 + 1, 1), :]
        left_top = left.astype(jnp.bfloat16).astype(jnp.float32)
        right_top = right.astype(jnp.bfloat16).astype(jnp.float32)
        mark = jnp.where(row == 0, left_top, jnp.where(row == 1, right_top, 0.0))
        mark = jnp.where(row == 2, left - left_top, jnp.where(row == 3, right - right_top, mark))
        out_ref[pl.ds(0, 16), pl.ds(hid, BLK)] = mark.astype(out_ref.dtype)
        out_ref[pl.ds(16, 112), pl.ds(hid, BLK)] = jnp.zeros((112, BLK), out_ref.dtype)


def fold_x_kernel(pos_ref, r1_ref, r2_ref, r3_ref, own_ref, kept_ref, o1_ref, o2_ref, o3_ref, total, bias):
    hid = total.shape[1]
    body, marks = pl.ds(0, hid), pl.ds(hid, BLK)
    refs = (r1_ref, r2_ref, r3_ref)
    total[...] = own_ref[:, body] + sum(ref[:, body].astype(jnp.float32) for ref in refs)
    top = pl.ds(0, 16)
    mark = own_ref[top, marks] + sum(ref[top, marks].astype(jnp.float32) for ref in refs)
    bias[pl.ds(0, 1), :] = mark[0:1] + mark[2:3]
    bias[pl.ds(1, 1), :] = mark[1:2] + mark[3:4]
    row = lax.broadcasted_iota(jnp.int32, (16, BLK), 0)
    for d, out_ref in enumerate((kept_ref, o1_ref, o2_ref, o3_ref)):
        to = lax.rem(pos_ref[1] + d, NZ)
        for kind in range(2):
            take = pl.ds(pl.multiple_of(kind * 64 + to * 16, 16), 16)
            out_ref[pl.ds(kind * 16, 16), body] = total[take, :].astype(out_ref.dtype)
        line = bias[pl.ds(to // 2, 1), :]
        high = line.astype(jnp.bfloat16).astype(jnp.float32)
        mark = jnp.where(row == 0, high, jnp.where(row == 1, line - high, 0.0))
        out_ref[top, marks] = mark.astype(out_ref.dtype)
        out_ref[pl.ds(16, 16), marks] = jnp.zeros((16, BLK), out_ref.dtype)


def last_kernel(pos_ref, r1_ref, r2_ref, r3_ref, own_ref, self_ref, neigh_ref, bias_ref):
    hid = self_ref.shape[1]
    body, marks = pl.ds(0, hid), pl.ds(hid, BLK)
    refs = (r1_ref, r2_ref, r3_ref)
    total = own_ref[:, body] + sum(ref[:, body].astype(jnp.float32) for ref in refs)
    top = pl.ds(0, 16)
    mark = own_ref[top, marks] + sum(ref[top, marks].astype(jnp.float32) for ref in refs)
    self_ref[...] = total[:16]
    neigh_ref[...] = total[16:]
    bias_ref[...] = jnp.broadcast_to(mark[0:1] + mark[1:2], (8, BLK))


def body(features, seed_feats, patterns, sources, counts, w_self, w_neigh, bias_term, out_grad):
    node = lax.axis_index("node")
    feat = lax.axis_index("feat")
    x, z, core = node // (NZ * 2), (node // 2) % NZ, node % 2
    y = feat % NY
    pos = jnp.stack([x, z, core, y]).astype(jnp.int32)
    hid = w_self.shape[1]
    swap = lambda value: lax.ppermute(value, "node", SWAP_CORE)

    packed = patterns.transpose(0, 1, 3, 2)
    table = jnp.concatenate([counts, sources.reshape(-1)])
    packed_other, table_other = swap(packed), swap(table)
    other = swap(jnp.where(core == 0, features[:, HALF:], features[:, :HALF]))
    lists = counts.shape[0]
    table = jnp.concatenate([table[:lists], table_other[:lists], table[lists:], table_other[lists:]])

    made = {}
    for d in (2, 1, 3, 0):
        meta = jnp.concatenate([jnp.stack([(x + d) % NX, core]).astype(jnp.int32), table])
        made[d] = sums(d > 0, meta, packed, packed_other, features, other)
    far = [lax.ppermute(made[d], "node", shift_x(d)) for d in (1, 2, 3)]

    seed_feats, w_self, bias_term, out_grad, own = lax.optimization_barrier(
        (seed_feats, w_self, bias_term, out_grad, made[0])
    )
    turned = seed_feats.T.reshape(WIDE // 32, 2, 16, BLK)
    pick = lambda c: lax.dynamic_index_in_dim(turned, c, 1, keepdims=False).reshape(HALF, BLK)
    seed_mine, seed_other = pick(core), swap(pick(1 - core))
    og_other = swap(out_grad)
    self_term = jnp.dot(seed_feats, w_self, preferred_element_type=jnp.float32)
    self_term = self_term + jnp.where(feat == 0, bias_term, 0.0)
    ready = (seed_mine, seed_other, og_other, self_term)

    own, *coded = call(merge_x_kernel, "merge_x", [SUM_PLAIN] + [SUM_CODED] * 3, 4, waits=len(ready))(
        pos, *far, own, *ready
    )
    arrived = [lax.ppermute(coded[d - 1], "node", shift_z(d)) for d in (2, 1, 3)]
    mine, give, rest = call(
        merge_z_kernel, "merge_z", [HALF16, shaped(HALF + BLK, BLK, jnp.bfloat16), shaped(BLK, BLK, jnp.bfloat16)], 4
    )(pos, *arrived, own)

    *coded, agg_mine, agg_other = call(
        pre_kernel, "pre_terms", [PLAIN] + [CODED] * 3 + [HALF16] * 2, 5,
        [pltpu.VMEM((WIDE, BLK), jnp.bfloat16), pltpu.VMEM((hid, BLK), jnp.float32)],
    )(pos, mine, swap(give), rest, w_neigh, self_term)
    own, *coded = coded
    received = [lax.ppermute(coded[d - 1], "feat", shift_y(d)) for d in (2, 1, 3)]
    (coded,) = call(merge_y_kernel, "merge_y", [CODED], 4)(pos, *received, own)
    far = lax.ppermute(coded, "feat", SWAP_FAR)
    (own,) = call(hidden_kernel, "hidden", [HALF16], 2)(pos, coded, far)
    chunks = [own] + [lax.ppermute(own, "feat", shift_y(d)) for d in (1, 2, 3)]
    chunks_other = [swap(chunk) for chunk in chunks]

    wide = hid + BLK
    scratch = [
        pltpu.VMEM((2 * BLK, hid), jnp.bfloat16),
        pltpu.VMEM((HALF, hid), jnp.float32),
        pltpu.VMEM((HALF, hid), jnp.float32),
        pltpu.VMEM((8, BLK), jnp.float32),
    ]
    outs = [shaped(BLK, hid, jnp.bfloat16), shaped(BLK, wide, jnp.float32)] + [shaped(BLK, wide, jnp.bfloat16)] * 3
    hidden, own, *parts = call(grads_kernel, "grads", outs, 14, scratch)(
        pos, *chunks, *chunks_other, out_grad, og_other, agg_mine, agg_other, seed_mine, seed_other
    )
    received = [lax.ppermute(parts[d - 1], "node", shift_x(d)) for d in (2, 1, 3)]
    own, *parts = call(
        fold_x_kernel, "fold_x", [shaped(32, wide, jnp.float32)] + [shaped(32, wide, jnp.bfloat16)] * 3, 4,
        [pltpu.VMEM((BLK, hid), jnp.float32), pltpu.VMEM((8, BLK), jnp.float32)],
    )(pos, *received, own)
    received = [lax.ppermute(parts[d - 1], "node", shift_z(d)) for d in (2, 1, 3)]
    part = shaped(16, hid, jnp.float32)
    grad_self, grad_neigh, bias = call(last_kernel, "last", [part, part, shaped(8, BLK, jnp.float32)], 4)(
        pos, *received, own
    )
    grad_bias = lax.dynamic_slice(bias[0], (z % 2 * 64 + core * 32,), (32,))
    return (hidden, grad_self, grad_neigh, grad_bias)


def solution(mesh):
    return jax.shard_map(
        body,
        mesh=mesh,
        in_specs=(
            P("node", "feat"),
            P("node", "feat"),
            P("node", None, None, None),
            P("node", None),
            P("node"),
            P("feat", None),
            P("feat", None),
            P(),
            P("node", None),
        ),
        out_specs=(
            P("node", None),
            P(("feat", "node"), None),
            P(("feat", "node"), None),
            P("node"),
        ),
        check_vma=False,
    )
```

```python
import functools

import jax
import jax.numpy as jnp
from jax import lax
from jax.experimental import pallas as pl
from jax.experimental.pallas import tpu as pltpu
from jax.sharding import PartitionSpec as P

BLK = 128
HALF = 256
FAN = 8
TOP = 32700.0
NX, NZ, NY = 4, 4, 4
WIDE = 512
VMEM = pl.BlockSpec(memory_space=pltpu.VMEM)
SMEM = pl.BlockSpec(memory_space=pltpu.SMEM)
PARAMS = pltpu.CompilerParams(vmem_limit_bytes=40 * 1024 * 1024)
F32 = functools.partial(lax.dot_general, preferred_element_type=jnp.float32)


def node_of(x, z, c):
    return x * (NZ * 2) + z * 2 + c


NODES = [(x, z, c) for x in range(NX) for z in range(NZ) for c in range(2)]
SWAP_CORE = [(n, n ^ 1) for n in range(NX * NZ * 2)]
SWAP_FAR = [(f, f ^ 4) for f in range(8)]


def shift_x(d):
    return [(node_of(x, z, c), node_of((x + d) % NX, z, c)) for x, z, c in NODES]


def shift_z(d):
    return [(node_of(x, z, c), node_of(x, (z + d) % NZ, c)) for x, z, c in NODES]


def shift_y(d):
    return [(h * 4 + y, h * 4 + (y + d) % NY) for h in range(2) for y in range(NY)]


def step_of(mantissa, exponent):
    return mantissa * jnp.exp2(exponent)


def encode(sums, count):
    top = jnp.maximum(jnp.max(jnp.abs(sums), axis=0, keepdims=True), 1e-25) * (1.0 / TOP)
    exponent = jnp.floor(jnp.log2(top)) - 13.0
    mantissa = jnp.ceil(top * jnp.exp2(-exponent))
    coded = jnp.round(sums * (1.0 / step_of(mantissa, exponent))).astype(jnp.int32).astype(jnp.int16)
    row = lax.broadcasted_iota(jnp.int32, (16, BLK), 0)
    tail = jnp.where(row == 0, count, jnp.where(row == 1, exponent, jnp.where(row == 2, mantissa, 0.0)))
    return coded, tail.astype(jnp.int32).astype(jnp.int16)


def put_coded(ref, sums, count):
    rows = sums.shape[0]
    coded, tail = encode(sums, count)
    ref[pl.ds(0, rows), :] = coded
    ref[pl.ds(rows, 16), :] = tail


def put_plain(ref, sums, count):
    rows = sums.shape[0]
    ref[pl.ds(0, rows), :] = sums
    ref[pl.ds(rows, 8), :] = jnp.broadcast_to(count, (8, BLK))


def plain(ref):
    rows = ref.shape[0] - 8
    return ref[pl.ds(0, rows), :], ref[pl.ds(rows, 8), :][0:1]


def decode(ref):
    rows = ref.shape[0] - 16
    tail = ref[pl.ds(rows, 16), :].astype(jnp.int32).astype(jnp.float32)
    values = ref[pl.ds(0, rows), :].astype(jnp.int32).astype(jnp.float32)
    return values * step_of(tail[2:3], tail[1:2]), tail[0:1]


def gathered(plain_refs, coded_refs):
    pairs = [plain(ref) for ref in plain_refs] + [decode(ref) for ref in coded_refs]
    return sum(pair[0] for pair in pairs), sum(pair[1] for pair in pairs)


def half_kernel(side_ref, features_ref, out_ref, done):
    parts = done.shape[0]
    step = out_ref.shape[0] // parts
    cols = pl.ds(pl.multiple_of(side_ref[0] * HALF, HALF), HALF)
    copies = []
    for part in range(parts):
        rows = pl.ds(part * step, step)
        copies.append(pltpu.make_async_copy(features_ref.at[rows, cols], out_ref.at[rows, :], done.at[part]))
    for copy in copies:
        copy.start()
    for copy in copies:
        copy.wait()


def half_columns(side, features):
    return pl.pallas_call(
        half_kernel,
        out_shape=jax.ShapeDtypeStruct((features.shape[0], HALF), features.dtype),
        in_specs=[SMEM, pl.BlockSpec(memory_space=pl.ANY)],
        out_specs=pl.BlockSpec(memory_space=pl.ANY),
        scratch_shapes=[pltpu.SemaphoreType.DMA((4,))],
        name="half_columns",
    )(side, features)


def sums_kernel(coded_out, meta_ref, pat0_ref, pat1_ref, feat0_ref, feat1_ref, even_ref, odd_ref, *scratch):
    tiles, accs, pops = scratch[0:2], scratch[2:4], scratch[4:7]
    pats, feats = (pat0_ref, pat1_ref), (feat0_ref, feat1_ref)
    blocks = pat0_ref.shape[0]
    slots = [(side, slot) for side in range(2) for slot in range(FAN)]
    put = put_coded if coded_out else put_plain

    def unpack(i, tile_ref, pop_ref):
        shifts = lax.broadcasted_iota(jnp.int32, (8, 16, BLK), 1)
        total = jnp.zeros((8, BLK), jnp.int32)
        for j, (side, slot) in enumerate(slots):
            live = meta_ref[2 + side * 32 + meta_ref[0] * blocks + i]
            words = pats[side][i, slot] * (slot < live).astype(jnp.int32)
            total += lax.population_count(words)
            bits = (jnp.broadcast_to(words[:, None, :], (8, 16, BLK)) >> shifts) & 1
            tile_ref[pl.ds(j * BLK, BLK), :] = bits.reshape(BLK, BLK).astype(jnp.float32).astype(jnp.bfloat16)
        pop_ref[...] = total

    def multiply(i, tile_ref, acc_ref):
        picked = []
        for side, slot in slots:
            source = meta_ref[66 + (side * 32 + meta_ref[0] * blocks + i) * FAN + slot]
            picked.append(feats[side][pl.ds(pl.multiple_of(source * BLK, BLK), BLK), :])
        acc_ref[...] = F32(tile_ref[...], jnp.concatenate(picked, axis=0), (((0,), (0,)), ((), ()))).T

    def finish(i, acc_ref, pop_ref):
        count = jnp.sum(pop_ref[...], axis=0, keepdims=True).astype(jnp.float32)
        put((even_ref, odd_ref)[i % 2].at[i // 2], acc_ref[...], count)

    for step in range(blocks + 2):
        if step < blocks:
            unpack(step, tiles[step % 2], pops[step % 3])
        if 0 <= step - 1 < blocks:
            multiply(step - 1, tiles[(step - 1) % 2], accs[(step - 1) % 2])
        if 0 <= step - 2 < blocks:
            finish(step - 2, accs[(step - 2) % 2], pops[(step - 2) % 3])


def sums(coded_out, meta, pat0, pat1, feat0, feat1):
    blocks = 2 * NZ
    pats = pl.BlockSpec((blocks, FAN, 8, BLK), lambda i, m: (m[0], 0, 0, 0))
    rows, kind = (HALF + 16, jnp.int16) if coded_out else (HALF + 8, jnp.float32)
    return pl.pallas_call(
        functools.partial(sums_kernel, coded_out),
        out_shape=[jax.ShapeDtypeStruct((NZ, rows, BLK), kind)] * 2,
        grid_spec=pltpu.PrefetchScalarGridSpec(
            num_scalar_prefetch=1,
            grid=(1,),
            in_specs=[
                pats,
                pats,
                pl.BlockSpec((feat0.shape[0], HALF), lambda i, m: (0, m[1])),
                pl.BlockSpec(feat1.shape, lambda i, m: (0, 0)),
            ],
            out_specs=[pl.BlockSpec((NZ, rows, BLK), lambda i, m: (0, 0, 0))] * 2,
            scratch_shapes=[pltpu.VMEM((2 * FAN * BLK, BLK), jnp.bfloat16)] * 2
            + [pltpu.VMEM((HALF, BLK), jnp.float32)] * 2
            + [pltpu.VMEM((8, BLK), jnp.int32)] * 3,
        ),
        compiler_params=PARAMS,
        cost_estimate=pl.CostEstimate(flops=2_000_000_000, bytes_accessed=3_000_000, transcendentals=0),
        name="sums",
    )(meta, pat0, pat1, feat0, feat1)


def call(kernel, name, outs, count, scratch=(), waits=0):
    return pl.pallas_call(
        kernel,
        out_shape=outs,
        in_specs=[SMEM] + [VMEM] * count + [pl.BlockSpec(memory_space=pl.ANY)] * waits,
        out_specs=[VMEM] * len(outs),
        scratch_shapes=list(scratch),
        compiler_params=PARAMS,
        name=name,
    )


def shaped(*dims):
    return jax.ShapeDtypeStruct(dims[:-1], dims[-1])


SUM_CODED = shaped(2, HALF + 16, BLK, jnp.int16)
SUM_PLAIN = shaped(2, HALF + 8, BLK, jnp.float32)
CODED = shaped(HALF + 16, BLK, jnp.int16)
PLAIN = shaped(HALF + 8, BLK, jnp.float32)
HALF16 = shaped(HALF, BLK, jnp.bfloat16)


def merge_x_kernel(pos_ref, *rest):
    for d, out_ref in enumerate(rest[-4:]):
        for c in range(2):
            index = lax.rem(pos_ref[1] + d, NZ)
            total, count = gathered((rest[6 + c].at[index],), [ref.at[index] for ref in rest[c:6:2]])
            (put_coded if d else put_plain)(out_ref.at[c], total, count)


def merge_z_kernel(pos_ref, r1_ref, r2_ref, r3_ref, own_ref, mine_ref, give_ref, rest_ref):
    core = pos_ref[2]
    for out_ref, index in ((mine_ref, core), (give_ref, 1 - core)):
        total, count = gathered((own_ref.at[index],), [ref.at[index] for ref in (r1_ref, r2_ref, r3_ref)])
        out_ref[pl.ds(0, HALF), :] = (total / jnp.sqrt(1.0 + count)).astype(jnp.bfloat16)
    for block in range(HALF // 32):
        keep = pl.ds(pl.multiple_of(block * 32 + core * 16, 16), 16)
        give = pl.ds(pl.multiple_of(block * 32 + 16 - core * 16, 16), 16)
        give_ref[pl.ds(HALF + block * 16, 16), :] = mine_ref[give, :]
        rest_ref[pl.ds(block * 16, 16), :] = give_ref[keep, :]


def pre_kernel(
    pos_ref, mine_ref, got_ref, rest_ref, w_ref, self_ref, own_ref, o1_ref, o2_ref, o3_ref, agg0_ref, agg1_ref, agg, acc
):
    core = pos_ref[2]
    agg[pl.ds(pl.multiple_of(core * HALF, HALF), HALF), :] = mine_ref[...]
    agg[pl.ds(pl.multiple_of((1 - core) * HALF, HALF), HALF), :] = got_ref[pl.ds(0, HALF), :]
    acc[...] = (self_ref[...] + F32(agg[...], w_ref[...], (((0,), (0,)), ((), ())))).T
    for d, out_ref in enumerate((own_ref, o1_ref, o2_ref, o3_ref)):
        terms = acc[pl.ds(pl.multiple_of(lax.rem(pos_ref[3] + d, NY) * HALF, HALF), HALF), :]
        (put_coded if d else put_plain)(out_ref, terms, jnp.zeros((1, BLK), jnp.float32))
    for block in range(WIDE // 32):
        rows = pl.ds(pl.multiple_of(block * 32 + core * 16, 16), 16)
        agg0_ref[pl.ds(block * 16, 16), :] = agg[rows, :]
    agg1_ref[pl.ds(pl.multiple_of(core * BLK, BLK), BLK), :] = rest_ref[...]
    agg1_ref[pl.ds(pl.multiple_of((1 - core) * BLK, BLK), BLK), :] = got_ref[pl.ds(HALF, BLK), :]


def merge_y_kernel(pos_ref, r1_ref, r2_ref, r3_ref, own_ref, out_ref):
    total, count = gathered((own_ref,), (r1_ref, r2_ref, r3_ref))
    put_coded(out_ref, total, count)


def hidden_kernel(pos_ref, own_ref, far_ref, out_ref):
    out_ref[...] = jnp.maximum(decode(own_ref)[0] + decode(far_ref)[0], 0.0).astype(jnp.bfloat16)


def grads_kernel(
    pos_ref, a0_ref, a1_ref, a2_ref, a3_ref, b0_ref, b1_ref, b2_ref, b3_ref, og0_ref, og1_ref,
    agg0_ref, agg1_ref, seed0_ref, seed1_ref,
    hidden_ref, own_ref, o1_ref, o2_ref, o3_ref, rows, self_acc, neigh_acc, bias,
):
    x, y = pos_ref[0], pos_ref[3]
    zero = jnp.zeros((BLK, HALF), jnp.bfloat16)
    for d in range(NY):
        place = pl.ds(pl.multiple_of(lax.rem(y + NY - d, NY) * HALF, HALF), HALF)
        for side, (refs, og_ref) in enumerate(
            (((a0_ref, a1_ref, a2_ref, a3_ref), og0_ref), ((b0_ref, b1_ref, b2_ref, b3_ref), og1_ref))
        ):
            value = refs[d][...].T
            if side == 0:
                hidden_ref[:, place] = value
            rows[pl.ds(side * BLK, BLK), place] = jnp.where(value > 0, og_ref[:, place], zero)
    hid = rows.shape[1]
    contract = (((1,), (0,)), ((), ()))
    self_acc[...] = F32(jnp.concatenate([seed0_ref[...], seed1_ref[...]], axis=1), rows[...], contract)
    neigh_acc[...] = F32(jnp.concatenate([agg0_ref[...], agg1_ref[...]], axis=1), rows[...], contract)
    total = F32(jnp.ones((8, 2 * BLK), jnp.bfloat16), rows[...], contract)[0:1]
    for part in range(hid // BLK):
        bias[pl.ds(part, 1), :] = total[:, part * BLK:(part + 1) * BLK]
    row = lax.broadcasted_iota(jnp.int32, (16, BLK), 0)
    for d, out_ref in enumerate((own_ref, o1_ref, o2_ref, o3_ref)):
        to = lax.rem(x + d, NX)
        take = pl.ds(pl.multiple_of(to * 64, 64), 64)
        out_ref[pl.ds(0, 64), pl.ds(0, hid)] = self_acc[take, :].astype(out_ref.dtype)
        out_ref[pl.ds(64, 64), pl.ds(0, hid)] = neigh_acc[take, :].astype(out_ref.dtype)
        left, right = bias[pl.ds(to * 2, 1), :], bias[pl.ds(to * 2 + 1, 1), :]
        left_top = left.astype(jnp.bfloat16).astype(jnp.float32)
        right_top = right.astype(jnp.bfloat16).astype(jnp.float32)
        mark = jnp.where(row == 0, left_top, jnp.where(row == 1, right_top, 0.0))
        mark = jnp.where(row == 2, left - left_top, jnp.where(row == 3, right - right_top, mark))
        out_ref[pl.ds(0, 16), pl.ds(hid, BLK)] = mark.astype(out_ref.dtype)
        out_ref[pl.ds(16, 112), pl.ds(hid, BLK)] = jnp.zeros((112, BLK), out_ref.dtype)


def fold_x_kernel(pos_ref, r1_ref, r2_ref, r3_ref, own_ref, kept_ref, o1_ref, o2_ref, o3_ref, total, bias):
    hid = total.shape[1]
    body, marks = pl.ds(0, hid), pl.ds(hid, BLK)
    refs = (r1_ref, r2_ref, r3_ref)
    total[...] = own_ref[:, body] + sum(ref[:, body].astype(jnp.float32) for ref in refs)
    top = pl.ds(0, 16)
    mark = own_ref[top, marks] + sum(ref[top, marks].astype(jnp.float32) for ref in refs)
    bias[pl.ds(0, 1), :] = mark[0:1] + mark[2:3]
    bias[pl.ds(1, 1), :] = mark[1:2] + mark[3:4]
    row = lax.broadcasted_iota(jnp.int32, (16, BLK), 0)
    for d, out_ref in enumerate((kept_ref, o1_ref, o2_ref, o3_ref)):
        to = lax.rem(pos_ref[1] + d, NZ)
        for kind in range(2):
            take = pl.ds(pl.multiple_of(kind * 64 + to * 16, 16), 16)
            out_ref[pl.ds(kind * 16, 16), body] = total[take, :].astype(out_ref.dtype)
        line = bias[pl.ds(to // 2, 1), :]
        high = line.astype(jnp.bfloat16).astype(jnp.float32)
        mark = jnp.where(row == 0, high, jnp.where(row == 1, line - high, 0.0))
        out_ref[top, marks] = mark.astype(out_ref.dtype)
        out_ref[pl.ds(16, 16), marks] = jnp.zeros((16, BLK), out_ref.dtype)


def last_kernel(pos_ref, r1_ref, r2_ref, r3_ref, own_ref, self_ref, neigh_ref, bias_ref):
    hid = self_ref.shape[1]
    body, marks = pl.ds(0, hid), pl.ds(hid, BLK)
    refs = (r1_ref, r2_ref, r3_ref)
    total = own_ref[:, body] + sum(ref[:, body].astype(jnp.float32) for ref in refs)
    top = pl.ds(0, 16)
    mark = own_ref[top, marks] + sum(ref[top, marks].astype(jnp.float32) for ref in refs)
    self_ref[...] = total[:16]
    neigh_ref[...] = total[16:]
    line = mark[0:1] + mark[1:2]
    for place in range(BLK // 32):
        @pl.when(lax.rem(pos_ref[1], 2) * 2 + pos_ref[2] == place)
        def _():
            bias_ref[...] = line[:, place * 32:place * 32 + 32]


def body(features, seed_feats, patterns, sources, counts, w_self, w_neigh, bias_term, out_grad):
    node = lax.axis_index("node")
    feat = lax.axis_index("feat")
    x, z, core = node // (NZ * 2), (node // 2) % NZ, node % 2
    y = feat % NY
    pos = jnp.stack([x, z, core, y]).astype(jnp.int32)
    hid = w_self.shape[1]
    swap = lambda value: lax.ppermute(value, "node", SWAP_CORE)

    packed = patterns.transpose(0, 1, 3, 2)
    table = jnp.concatenate([counts, sources.reshape(-1)])
    packed_other, table_other = swap(packed), swap(table)
    other = swap(half_columns((1 - core)[None].astype(jnp.int32), features))
    lists = counts.shape[0]
    table = jnp.concatenate([table[:lists], table_other[:lists], table[lists:], table_other[lists:]])

    made = {}
    for d in (2, 1, 3, 0):
        meta = jnp.concatenate([jnp.stack([(x + d) % NX, core]).astype(jnp.int32), table])
        made[d] = sums(d > 0, meta, packed, packed_other, features, other)
    far = [lax.ppermute(part, "node", shift_x(d)) for d in (2, 1, 3) for part in made[d]]

    seed_feats, w_self, bias_term, out_grad, own = lax.optimization_barrier(
        (seed_feats, w_self, bias_term, out_grad, made[0])
    )
    turned = seed_feats.T.reshape(WIDE // 32, 2, 16, BLK)
    pick = lambda c: lax.dynamic_index_in_dim(turned, c, 1, keepdims=False).reshape(HALF, BLK)
    seed_mine, seed_other = pick(core), swap(pick(1 - core))
    og_other = swap(out_grad)
    self_term = jnp.dot(seed_feats, w_self, preferred_element_type=jnp.float32)
    self_term = self_term + jnp.where(feat == 0, bias_term, 0.0)

    own, *coded = call(merge_x_kernel, "merge_x", [SUM_PLAIN] + [SUM_CODED] * 3, 8)(
        pos, *far, *own
    )
    arrived = [lax.ppermute(coded[d - 1], "node", shift_z(d)) for d in (2, 1, 3)]
    mine, give, rest = call(
        merge_z_kernel, "merge_z", [HALF16, shaped(HALF + BLK, BLK, jnp.bfloat16), shaped(BLK, BLK, jnp.bfloat16)], 4
    )(pos, *arrived, own)

    *coded, agg_mine, agg_other = call(
        pre_kernel, "pre_terms", [PLAIN] + [CODED] * 3 + [HALF16] * 2, 5,
        [pltpu.VMEM((WIDE, BLK), jnp.bfloat16), pltpu.VMEM((hid, BLK), jnp.float32)],
    )(pos, mine, swap(give), rest, w_neigh, self_term)
    own, *coded = coded
    received = [lax.ppermute(coded[d - 1], "feat", shift_y(d)) for d in (2, 1, 3)]
    (coded,) = call(merge_y_kernel, "merge_y", [CODED], 4)(pos, *received, own)
    far = lax.ppermute(coded, "feat", SWAP_FAR)
    (own,) = call(hidden_kernel, "hidden", [HALF16], 2)(pos, coded, far)
    chunks = [own] + [lax.ppermute(own, "feat", shift_y(d)) for d in (1, 2, 3)]
    chunks_other = [swap(chunk) for chunk in chunks]

    wide = hid + BLK
    scratch = [
        pltpu.VMEM((2 * BLK, hid), jnp.bfloat16),
        pltpu.VMEM((HALF, hid), jnp.float32),
        pltpu.VMEM((HALF, hid), jnp.float32),
        pltpu.VMEM((8, BLK), jnp.float32),
    ]
    outs = [shaped(BLK, hid, jnp.bfloat16), shaped(BLK, wide, jnp.float32)] + [shaped(BLK, wide, jnp.bfloat16)] * 3
    hidden, own, *parts = call(grads_kernel, "grads", outs, 14, scratch)(
        pos, *chunks, *chunks_other, out_grad, og_other, agg_mine, agg_other, seed_mine, seed_other
    )
    received = [lax.ppermute(parts[d - 1], "node", shift_x(d)) for d in (2, 1, 3)]
    own, *parts = call(
        fold_x_kernel, "fold_x", [shaped(32, wide, jnp.float32)] + [shaped(32, wide, jnp.bfloat16)] * 3, 4,
        [pltpu.VMEM((BLK, hid), jnp.float32), pltpu.VMEM((8, BLK), jnp.float32)],
    )(pos, *received, own)
    received = [lax.ppermute(parts[d - 1], "node", shift_z(d)) for d in (2, 1, 3)]
    part = shaped(16, hid, jnp.float32)
    grad_self, grad_neigh, bias = call(last_kernel, "last", [part, part, shaped(1, 32, jnp.float32)], 4)(
        pos, *received, own
    )
    return (hidden, grad_self, grad_neigh, bias[0])


def solution(mesh):
    return jax.shard_map(
        body,
        mesh=mesh,
        in_specs=(
            P("node", "feat"),
            P("node", "feat"),
            P("node", None, None, None),
            P("node", None),
            P("node"),
            P("feat", None),
            P("feat", None),
            P(),
            P("node", None),
        ),
        out_specs=(
            P("node", None),
            P(("feat", "node"), None),
            P(("feat", "node"), None),
            P("node"),
        ),
        check_vma=False,
    )
```

```python
import functools

import jax
import jax.numpy as jnp
from jax import lax
from jax.experimental import pallas as pl
from jax.experimental.pallas import tpu as pltpu
from jax.sharding import PartitionSpec as P

BLK = 128
HALF = 256
FAN = 8
TOP = 32700.0
NX, NZ, NY = 4, 4, 4
WIDE = 512
VMEM = pl.BlockSpec(memory_space=pltpu.VMEM)
SMEM = pl.BlockSpec(memory_space=pltpu.SMEM)
PARAMS = pltpu.CompilerParams(vmem_limit_bytes=40 * 1024 * 1024)
ALONE = pltpu.CompilerParams(vmem_limit_bytes=63 * 1024 * 1024)
F32 = functools.partial(lax.dot_general, preferred_element_type=jnp.float32)


def node_of(x, z, c):
    return x * (NZ * 2) + z * 2 + c


NODES = [(x, z, c) for x in range(NX) for z in range(NZ) for c in range(2)]
SWAP_CORE = [(n, n ^ 1) for n in range(NX * NZ * 2)]
SWAP_FAR = [(f, f ^ 4) for f in range(8)]


def shift_x(d):
    return [(node_of(x, z, c), node_of((x + d) % NX, z, c)) for x, z, c in NODES]


def shift_z(d):
    return [(node_of(x, z, c), node_of(x, (z + d) % NZ, c)) for x, z, c in NODES]


def shift_y(d):
    return [(h * 4 + y, h * 4 + (y + d) % NY) for h in range(2) for y in range(NY)]


def step_of(mantissa, exponent):
    return mantissa * jnp.exp2(exponent)


def encode(sums, count):
    top = jnp.maximum(jnp.max(jnp.abs(sums), axis=0, keepdims=True), 1e-25) * (1.0 / TOP)
    exponent = jnp.floor(jnp.log2(top)) - 13.0
    mantissa = jnp.ceil(top * jnp.exp2(-exponent))
    coded = jnp.round(sums * (1.0 / step_of(mantissa, exponent))).astype(jnp.int32).astype(jnp.int16)
    row = lax.broadcasted_iota(jnp.int32, (16, BLK), 0)
    tail = jnp.where(row == 0, count, jnp.where(row == 1, exponent, jnp.where(row == 2, mantissa, 0.0)))
    return coded, tail.astype(jnp.int32).astype(jnp.int16)


def put_coded(ref, sums, count):
    rows = sums.shape[0]
    coded, tail = encode(sums, count)
    ref[pl.ds(0, rows), :] = coded
    ref[pl.ds(rows, 16), :] = tail


def put_plain(ref, sums, count):
    rows = sums.shape[0]
    ref[pl.ds(0, rows), :] = sums
    ref[pl.ds(rows, 8), :] = jnp.broadcast_to(count, (8, BLK))


def plain(ref):
    rows = ref.shape[0] - 8
    return ref[pl.ds(0, rows), :], ref[pl.ds(rows, 8), :][0:1]


def decode(ref):
    rows = ref.shape[0] - 16
    tail = ref[pl.ds(rows, 16), :].astype(jnp.int32).astype(jnp.float32)
    values = ref[pl.ds(0, rows), :].astype(jnp.int32).astype(jnp.float32)
    return values * step_of(tail[2:3], tail[1:2]), tail[0:1]


def gathered(plain_refs, coded_refs):
    pairs = [plain(ref) for ref in plain_refs] + [decode(ref) for ref in coded_refs]
    return sum(pair[0] for pair in pairs), sum(pair[1] for pair in pairs)


def half_kernel(side_ref, features_ref, out_ref, held, came, went):
    parts = came.shape[0]
    step = held.shape[0] // parts
    cols = pl.ds(pl.multiple_of(side_ref[0] * HALF, HALF), HALF)
    take, give = [], []
    for part in range(parts):
        rows = pl.ds(part * step, step)
        take.append(pltpu.make_async_copy(features_ref.at[rows, cols], held.at[rows, :], came.at[part]))
        give.append(pltpu.make_async_copy(held.at[rows, :], out_ref.at[rows, :], went.at[part]))
    for copy in take:
        copy.start()
    for part in range(parts):
        take[part].wait()
        give[part].start()
    for copy in give:
        copy.wait()


def half_columns(side, features):
    nodes = features.shape[0]
    return pl.pallas_call(
        half_kernel,
        out_shape=jax.ShapeDtypeStruct((nodes, HALF), features.dtype),
        in_specs=[SMEM, pl.BlockSpec(memory_space=pl.ANY)],
        out_specs=pl.BlockSpec(memory_space=pl.ANY),
        scratch_shapes=[pltpu.VMEM((nodes, HALF), features.dtype)] + [pltpu.SemaphoreType.DMA((8,))] * 2,
        compiler_params=ALONE,
        name="half_columns",
    )(side, features)


def sums_kernel(d, pos_ref, table_ref, pat0_ref, pat1_ref, feat0_ref, feat1_ref, even_ref, odd_ref, *scratch):
    tiles, accs, pops, pats, feats, done = scratch[0:2], scratch[2:4], scratch[4:7], scratch[7:9], scratch[9:11], scratch[11]
    blocks = pats[0].shape[0]
    first = lax.rem(pos_ref[0] + d, NX) * blocks
    group = pl.ds(first, blocks)
    half = pl.ds(pl.multiple_of(pos_ref[2] * HALF, HALF), HALF)
    copies = [
        pltpu.make_async_copy(pat0_ref.at[group], pats[0], done.at[0]),
        pltpu.make_async_copy(pat1_ref.at[group], pats[1], done.at[1]),
        pltpu.make_async_copy(feat0_ref.at[:, half], feats[0], done.at[2]),
        pltpu.make_async_copy(feat1_ref, feats[1], done.at[3]),
    ]
    for copy in copies:
        copy.start()
    copies[0].wait()
    copies[1].wait()
    slots = [(side, slot) for side in range(2) for slot in range(FAN)]
    put = put_coded if d else put_plain

    def unpack(i, tile_ref, pop_ref):
        shifts = lax.broadcasted_iota(jnp.int32, (8, 16, BLK), 1)
        total = jnp.zeros((8, BLK), jnp.int32)
        for j, (side, slot) in enumerate(slots):
            live = table_ref[side * 32 + first + i]
            words = pats[side][i, slot] * (slot < live).astype(jnp.int32)
            total += lax.population_count(words)
            bits = (jnp.broadcast_to(words[:, None, :], (8, 16, BLK)) >> shifts) & 1
            tile_ref[pl.ds(j * BLK, BLK), :] = bits.reshape(BLK, BLK).astype(jnp.float32).astype(jnp.bfloat16)
        pop_ref[...] = total

    def multiply(i, tile_ref, acc_ref):
        picked = []
        for side, slot in slots:
            source = table_ref[64 + (side * 32 + first + i) * FAN + slot]
            picked.append(feats[side][pl.ds(pl.multiple_of(source * BLK, BLK), BLK), :])
        acc_ref[...] = F32(tile_ref[...], jnp.concatenate(picked, axis=0), (((0,), (0,)), ((), ()))).T

    def finish(i, acc_ref, pop_ref):
        count = jnp.sum(pop_ref[...], axis=0, keepdims=True).astype(jnp.float32)
        put((even_ref, odd_ref)[i % 2].at[i // 2], acc_ref[...], count)

    for step in range(blocks + 2):
        if step < blocks:
            unpack(step, tiles[step % 2], pops[step % 3])
        if step == 0:
            copies[2].wait()
            copies[3].wait()
        if 0 <= step - 1 < blocks:
            multiply(step - 1, tiles[(step - 1) % 2], accs[(step - 1) % 2])
        if 0 <= step - 2 < blocks:
            finish(step - 2, accs[(step - 2) % 2], pops[(step - 2) % 3])


def sums(d, pos, table, pat0, pat1, feat0, feat1):
    blocks = 2 * NZ
    rows, kind = (HALF + 16, jnp.int16) if d else (HALF + 8, jnp.float32)
    nodes = feat0.shape[0]
    return pl.pallas_call(
        functools.partial(sums_kernel, d),
        out_shape=[jax.ShapeDtypeStruct((NZ, rows, BLK), kind)] * 2,
        in_specs=[SMEM] * 2 + [pl.BlockSpec(memory_space=pl.ANY)] * 4,
        out_specs=[VMEM] * 2,
        scratch_shapes=[pltpu.VMEM((2 * FAN * BLK, BLK), jnp.bfloat16)] * 2
        + [pltpu.VMEM((HALF, BLK), jnp.float32)] * 2
        + [pltpu.VMEM((8, BLK), jnp.int32)] * 3
        + [pltpu.VMEM((blocks,) + pat0.shape[1:], jnp.int32)] * 2
        + [pltpu.VMEM((nodes, HALF), jnp.bfloat16)] * 2
        + [pltpu.SemaphoreType.DMA((4,))],
        compiler_params=ALONE,
        cost_estimate=pl.CostEstimate(flops=2_000_000_000, bytes_accessed=3_000_000, transcendentals=0),
        name="sums",
    )(pos, table, pat0, pat1, feat0, feat1)


def call(kernel, name, outs, count, scratch=(), waits=0, params=PARAMS):
    return pl.pallas_call(
        kernel,
        out_shape=outs,
        in_specs=[SMEM] + [VMEM] * count + [pl.BlockSpec(memory_space=pl.ANY)] * waits,
        out_specs=[VMEM] * len(outs),
        scratch_shapes=list(scratch),
        compiler_params=params,
        name=name,
    )


def shaped(*dims):
    return jax.ShapeDtypeStruct(dims[:-1], dims[-1])


SUM_CODED = shaped(2, HALF + 16, BLK, jnp.int16)
SUM_PLAIN = shaped(2, HALF + 8, BLK, jnp.float32)
CODED = shaped(HALF + 16, BLK, jnp.int16)
PLAIN = shaped(HALF + 8, BLK, jnp.float32)
HALF16 = shaped(HALF, BLK, jnp.bfloat16)


def merge_x_kernel(pos_ref, *rest):
    for d, out_ref in enumerate(rest[-4:]):
        for c in range(2):
            index = lax.rem(pos_ref[1] + d, NZ)
            total, count = gathered((rest[6 + c].at[index],), [ref.at[index] for ref in rest[c:6:2]])
            (put_coded if d else put_plain)(out_ref.at[c], total, count)


def merge_z_kernel(pos_ref, r1_ref, r2_ref, r3_ref, own_ref, *rest):
    mine_ref, give_ref, rest_ref = rest[-3:]
    core = pos_ref[2]
    for out_ref, index in ((mine_ref, core), (give_ref, 1 - core)):
        total, count = gathered((own_ref.at[index],), [ref.at[index] for ref in (r1_ref, r2_ref, r3_ref)])
        out_ref[pl.ds(0, HALF), :] = (total / jnp.sqrt(1.0 + count)).astype(jnp.bfloat16)
    for block in range(HALF // 32):
        keep = pl.ds(pl.multiple_of(block * 32 + core * 16, 16), 16)
        give = pl.ds(pl.multiple_of(block * 32 + 16 - core * 16, 16), 16)
        give_ref[pl.ds(HALF + block * 16, 16), :] = mine_ref[give, :]
        rest_ref[pl.ds(block * 16, 16), :] = give_ref[keep, :]


def pre_kernel(
    pos_ref, mine_ref, got_ref, rest_ref, w_ref, self_ref, own_ref, o1_ref, o2_ref, o3_ref, agg0_ref, agg1_ref, agg, acc
):
    core = pos_ref[2]
    agg[pl.ds(pl.multiple_of(core * HALF, HALF), HALF), :] = mine_ref[...]
    agg[pl.ds(pl.multiple_of((1 - core) * HALF, HALF), HALF), :] = got_ref[pl.ds(0, HALF), :]
    acc[...] = (self_ref[...] + F32(agg[...], w_ref[...], (((0,), (0,)), ((), ())))).T
    for d, out_ref in enumerate((own_ref, o1_ref, o2_ref, o3_ref)):
        terms = acc[pl.ds(pl.multiple_of(lax.rem(pos_ref[3] + d, NY) * HALF, HALF), HALF), :]
        (put_coded if d else put_plain)(out_ref, terms, jnp.zeros((1, BLK), jnp.float32))
    for block in range(WIDE // 32):
        rows = pl.ds(pl.multiple_of(block * 32 + core * 16, 16), 16)
        agg0_ref[pl.ds(block * 16, 16), :] = agg[rows, :]
    agg1_ref[pl.ds(pl.multiple_of(core * BLK, BLK), BLK), :] = rest_ref[...]
    agg1_ref[pl.ds(pl.multiple_of((1 - core) * BLK, BLK), BLK), :] = got_ref[pl.ds(HALF, BLK), :]


def merge_y_kernel(pos_ref, r1_ref, r2_ref, r3_ref, own_ref, out_ref):
    total, count = gathered((own_ref,), (r1_ref, r2_ref, r3_ref))
    put_coded(out_ref, total, count)


def hidden_kernel(pos_ref, own_ref, far_ref, out_ref):
    out_ref[...] = jnp.maximum(decode(own_ref)[0] + decode(far_ref)[0], 0.0).astype(jnp.bfloat16)


def grads_kernel(
    pos_ref, a0_ref, a1_ref, a2_ref, a3_ref, b0_ref, b1_ref, b2_ref, b3_ref, og0_ref, og1_ref,
    agg0_ref, agg1_ref, seed0_ref, seed1_ref,
    hidden_ref, own_ref, o1_ref, o2_ref, o3_ref, rows, self_acc, neigh_acc, bias,
):
    x, y = pos_ref[0], pos_ref[3]
    zero = jnp.zeros((BLK, HALF), jnp.bfloat16)
    for d in range(NY):
        place = pl.ds(pl.multiple_of(lax.rem(y + NY - d, NY) * HALF, HALF), HALF)
        for side, (refs, og_ref) in enumerate(
            (((a0_ref, a1_ref, a2_ref, a3_ref), og0_ref), ((b0_ref, b1_ref, b2_ref, b3_ref), og1_ref))
        ):
            value = refs[d][...].T
            if side == 0:
                hidden_ref[:, place] = value
            rows[pl.ds(side * BLK, BLK), place] = jnp.where(value > 0, og_ref[:, place], zero)
    hid = rows.shape[1]
    contract = (((1,), (0,)), ((), ()))
    self_acc[...] = F32(jnp.concatenate([seed0_ref[...], seed1_ref[...]], axis=1), rows[...], contract)
    neigh_acc[...] = F32(jnp.concatenate([agg0_ref[...], agg1_ref[...]], axis=1), rows[...], contract)
    total = F32(jnp.ones((8, 2 * BLK), jnp.bfloat16), rows[...], contract)[0:1]
    for part in range(hid // BLK):
        bias[pl.ds(part, 1), :] = total[:, part * BLK:(part + 1) * BLK]
    row = lax.broadcasted_iota(jnp.int32, (16, BLK), 0)
    for d, out_ref in enumerate((own_ref, o1_ref, o2_ref, o3_ref)):
        to = lax.rem(x + d, NX)
        take = pl.ds(pl.multiple_of(to * 64, 64), 64)
        out_ref[pl.ds(0, 64), pl.ds(0, hid)] = self_acc[take, :].astype(out_ref.dtype)
        out_ref[pl.ds(64, 64), pl.ds(0, hid)] = neigh_acc[take, :].astype(out_ref.dtype)
        left, right = bias[pl.ds(to * 2, 1), :], bias[pl.ds(to * 2 + 1, 1), :]
        left_top = left.astype(jnp.bfloat16).astype(jnp.float32)
        right_top = right.astype(jnp.bfloat16).astype(jnp.float32)
        mark = jnp.where(row == 0, left_top, jnp.where(row == 1, right_top, 0.0))
        mark = jnp.where(row == 2, left - left_top, jnp.where(row == 3, right - right_top, mark))
        out_ref[pl.ds(0, 16), pl.ds(hid, BLK)] = mark.astype(out_ref.dtype)
        out_ref[pl.ds(16, 112), pl.ds(hid, BLK)] = jnp.zeros((112, BLK), out_ref.dtype)


def fold_x_kernel(pos_ref, r1_ref, r2_ref, r3_ref, own_ref, kept_ref, o1_ref, o2_ref, o3_ref, total, bias):
    hid = total.shape[1]
    body, marks = pl.ds(0, hid), pl.ds(hid, BLK)
    refs = (r1_ref, r2_ref, r3_ref)
    total[...] = own_ref[:, body] + sum(ref[:, body].astype(jnp.float32) for ref in refs)
    top = pl.ds(0, 16)
    mark = own_ref[top, marks] + sum(ref[top, marks].astype(jnp.float32) for ref in refs)
    bias[pl.ds(0, 1), :] = mark[0:1] + mark[2:3]
    bias[pl.ds(1, 1), :] = mark[1:2] + mark[3:4]
    row = lax.broadcasted_iota(jnp.int32, (16, BLK), 0)
    for d, out_ref in enumerate((kept_ref, o1_ref, o2_ref, o3_ref)):
        to = lax.rem(pos_ref[1] + d, NZ)
        for kind in range(2):
            take = pl.ds(pl.multiple_of(kind * 64 + to * 16, 16), 16)
            out_ref[pl.ds(kind * 16, 16), body] = total[take, :].astype(out_ref.dtype)
        line = bias[pl.ds(to // 2, 1), :]
        high = line.astype(jnp.bfloat16).astype(jnp.float32)
        mark = jnp.where(row == 0, high, jnp.where(row == 1, line - high, 0.0))
        out_ref[top, marks] = mark.astype(out_ref.dtype)
        out_ref[pl.ds(16, 16), marks] = jnp.zeros((16, BLK), out_ref.dtype)


def last_kernel(pos_ref, r1_ref, r2_ref, r3_ref, own_ref, self_ref, neigh_ref, bias_ref):
    hid = self_ref.shape[1]
    body, marks = pl.ds(0, hid), pl.ds(hid, BLK)
    refs = (r1_ref, r2_ref, r3_ref)
    total = own_ref[:, body] + sum(ref[:, body].astype(jnp.float32) for ref in refs)
    top = pl.ds(0, 16)
    mark = own_ref[top, marks] + sum(ref[top, marks].astype(jnp.float32) for ref in refs)
    self_ref[...] = total[:16]
    neigh_ref[...] = total[16:]
    line = mark[0:1] + mark[1:2]
    for place in range(BLK // 32):
        @pl.when(lax.rem(pos_ref[1], 2) * 2 + pos_ref[2] == place)
        def _():
            bias_ref[...] = line[:, place * 32:place * 32 + 32]


def body(features, seed_feats, patterns, sources, counts, w_self, w_neigh, bias_term, out_grad):
    node = lax.axis_index("node")
    feat = lax.axis_index("feat")
    x, z, core = node // (NZ * 2), (node // 2) % NZ, node % 2
    y = feat % NY
    pos = jnp.stack([x, z, core, y]).astype(jnp.int32)
    hid = w_self.shape[1]
    swap = lambda value: lax.ppermute(value, "node", SWAP_CORE)

    packed = patterns.transpose(0, 1, 3, 2)
    table = jnp.concatenate([counts, sources.reshape(-1)])
    packed_other, table_other = swap(packed), swap(table)
    other = swap(half_columns((1 - core)[None].astype(jnp.int32), features))
    lists = counts.shape[0]
    table = jnp.concatenate([table[:lists], table_other[:lists], table[lists:], table_other[lists:]])

    made = {}
    for d in (2, 1, 3, 0):
        made[d] = sums(d, pos, table, packed, packed_other, features, other)
    far = [lax.ppermute(part, "node", shift_x(d)) for d in (2, 1, 3) for part in made[d]]

    seed_feats, w_self, bias_term, out_grad, own = lax.optimization_barrier(
        (seed_feats, w_self, bias_term, out_grad, made[0])
    )
    turned = seed_feats.T.reshape(WIDE // 32, 2, 16, BLK)
    pick = lambda c: lax.dynamic_index_in_dim(turned, c, 1, keepdims=False).reshape(HALF, BLK)
    seed_mine, seed_other = pick(core), swap(pick(1 - core))
    og_other = swap(out_grad)
    self_term = jnp.dot(seed_feats, w_self, preferred_element_type=jnp.float32)
    self_term = self_term + jnp.where(feat == 0, bias_term, 0.0)

    own, *coded = call(merge_x_kernel, "merge_x", [SUM_PLAIN] + [SUM_CODED] * 3, 8, params=ALONE)(
        pos, *far, *own
    )
    arrived = [lax.ppermute(coded[d - 1], "node", shift_z(d)) for d in (2, 1, 3)]
    mine, give, rest = call(
        merge_z_kernel, "merge_z", [HALF16, shaped(HALF + BLK, BLK, jnp.bfloat16), shaped(BLK, BLK, jnp.bfloat16)], 4
    )(pos, *arrived, own)

    *coded, agg_mine, agg_other = call(
        pre_kernel, "pre_terms", [PLAIN] + [CODED] * 3 + [HALF16] * 2, 5,
        [pltpu.VMEM((WIDE, BLK), jnp.bfloat16), pltpu.VMEM((hid, BLK), jnp.float32)],
    )(pos, mine, swap(give), rest, w_neigh, self_term)
    own, *coded = coded
    received = [lax.ppermute(coded[d - 1], "feat", shift_y(d)) for d in (2, 1, 3)]
    (coded,) = call(merge_y_kernel, "merge_y", [CODED], 4)(pos, *received, own)
    far = lax.ppermute(coded, "feat", SWAP_FAR)
    (own,) = call(hidden_kernel, "hidden", [HALF16], 2)(pos, coded, far)
    chunks = [own] + [lax.ppermute(own, "feat", shift_y(d)) for d in (1, 2, 3)]
    chunks_other = [swap(chunk) for chunk in chunks]

    wide = hid + BLK
    scratch = [
        pltpu.VMEM((2 * BLK, hid), jnp.bfloat16),
        pltpu.VMEM((HALF, hid), jnp.float32),
        pltpu.VMEM((HALF, hid), jnp.float32),
        pltpu.VMEM((8, BLK), jnp.float32),
    ]
    outs = [shaped(BLK, hid, jnp.bfloat16), shaped(BLK, wide, jnp.float32)] + [shaped(BLK, wide, jnp.bfloat16)] * 3
    hidden, own, *parts = call(grads_kernel, "grads", outs, 14, scratch)(
        pos, *chunks, *chunks_other, out_grad, og_other, agg_mine, agg_other, seed_mine, seed_other
    )
    received = [lax.ppermute(parts[d - 1], "node", shift_x(d)) for d in (2, 1, 3)]
    own, *parts = call(
        fold_x_kernel, "fold_x", [shaped(32, wide, jnp.float32)] + [shaped(32, wide, jnp.bfloat16)] * 3, 4,
        [pltpu.VMEM((BLK, hid), jnp.float32), pltpu.VMEM((8, BLK), jnp.float32)],
    )(pos, *received, own)
    received = [lax.ppermute(parts[d - 1], "node", shift_z(d)) for d in (2, 1, 3)]
    part = shaped(16, hid, jnp.float32)
    grad_self, grad_neigh, bias = call(last_kernel, "last", [part, part, shaped(1, 32, jnp.float32)], 4)(
        pos, *received, own
    )
    return (hidden, grad_self, grad_neigh, bias[0])


def solution(mesh):
    return jax.shard_map(
        body,
        mesh=mesh,
        in_specs=(
            P("node", "feat"),
            P("node", "feat"),
            P("node", None, None, None),
            P("node", None),
            P("node"),
            P("feat", None),
            P("feat", None),
            P(),
            P("node", None),
        ),
        out_specs=(
            P("node", None),
            P(("feat", "node"), None),
            P(("feat", "node"), None),
            P("node"),
        ),
        check_vma=False,
    )
```

```python
import functools

import jax
import jax.numpy as jnp
from jax import lax
from jax.experimental import pallas as pl
from jax.experimental.pallas import tpu as pltpu
from jax.sharding import PartitionSpec as P

BLK = 128
HALF = 256
FAN = 8
TOP = 32700.0
NX, NZ, NY = 4, 4, 4
WIDE = 512
VMEM = pl.BlockSpec(memory_space=pltpu.VMEM)
SMEM = pl.BlockSpec(memory_space=pltpu.SMEM)
PARAMS = pltpu.CompilerParams(vmem_limit_bytes=40 * 1024 * 1024)
ALONE = pltpu.CompilerParams(vmem_limit_bytes=63 * 1024 * 1024)
F32 = functools.partial(lax.dot_general, preferred_element_type=jnp.float32)


def node_of(x, z, c):
    return x * (NZ * 2) + z * 2 + c


NODES = [(x, z, c) for x in range(NX) for z in range(NZ) for c in range(2)]
SWAP_CORE = [(n, n ^ 1) for n in range(NX * NZ * 2)]
SWAP_FAR = [(f, f ^ 4) for f in range(8)]


def shift_x(d):
    return [(node_of(x, z, c), node_of((x + d) % NX, z, c)) for x, z, c in NODES]


def shift_z(d):
    return [(node_of(x, z, c), node_of(x, (z + d) % NZ, c)) for x, z, c in NODES]


def shift_y(d):
    return [(h * 4 + y, h * 4 + (y + d) % NY) for h in range(2) for y in range(NY)]


def step_of(mantissa, exponent):
    return mantissa * jnp.exp2(exponent)


def encode(sums, count):
    top = jnp.maximum(jnp.max(jnp.abs(sums), axis=0, keepdims=True), 1e-25) * (1.0 / TOP)
    exponent = jnp.floor(jnp.log2(top)) - 13.0
    mantissa = jnp.ceil(top * jnp.exp2(-exponent))
    coded = jnp.round(sums * (1.0 / step_of(mantissa, exponent))).astype(jnp.int32).astype(jnp.int16)
    row = lax.broadcasted_iota(jnp.int32, (16, BLK), 0)
    tail = jnp.where(row == 0, count, jnp.where(row == 1, exponent, jnp.where(row == 2, mantissa, 0.0)))
    return coded, tail.astype(jnp.int32).astype(jnp.int16)


def put_coded(ref, sums, count):
    rows = sums.shape[0]
    coded, tail = encode(sums, count)
    ref[pl.ds(0, rows), :] = coded
    ref[pl.ds(rows, 16), :] = tail


def put_plain(ref, sums, count):
    rows = sums.shape[0]
    ref[pl.ds(0, rows), :] = sums
    ref[pl.ds(rows, 8), :] = jnp.broadcast_to(count, (8, BLK))


def plain(ref):
    rows = ref.shape[0] - 8
    return ref[pl.ds(0, rows), :], ref[pl.ds(rows, 8), :][0:1]


def decode(ref):
    rows = ref.shape[0] - 16
    tail = ref[pl.ds(rows, 16), :].astype(jnp.int32).astype(jnp.float32)
    values = ref[pl.ds(0, rows), :].astype(jnp.int32).astype(jnp.float32)
    return values * step_of(tail[2:3], tail[1:2]), tail[0:1]


def gathered(plain_refs, coded_refs):
    pairs = [plain(ref) for ref in plain_refs] + [decode(ref) for ref in coded_refs]
    return sum(pair[0] for pair in pairs), sum(pair[1] for pair in pairs)


def half_kernel(side_ref, features_ref, out_ref, held, came, went):
    parts = came.shape[0]
    step = held.shape[0] // parts
    cols = pl.ds(pl.multiple_of(side_ref[0] * HALF, HALF), HALF)
    take, give = [], []
    for part in range(parts):
        rows = pl.ds(part * step, step)
        take.append(pltpu.make_async_copy(features_ref.at[rows, cols], held.at[rows, :], came.at[part]))
        give.append(pltpu.make_async_copy(held.at[rows, :], out_ref.at[rows, :], went.at[part]))
    for copy in take:
        copy.start()
    for part in range(parts):
        take[part].wait()
        give[part].start()
    for copy in give:
        copy.wait()


def half_columns(side, features):
    nodes = features.shape[0]
    return pl.pallas_call(
        half_kernel,
        out_shape=jax.ShapeDtypeStruct((nodes, HALF), features.dtype),
        in_specs=[SMEM, pl.BlockSpec(memory_space=pl.ANY)],
        out_specs=pl.BlockSpec(memory_space=pl.ANY),
        scratch_shapes=[pltpu.VMEM((nodes, HALF), features.dtype)] + [pltpu.SemaphoreType.DMA((8,))] * 2,
        compiler_params=ALONE,
        name="half_columns",
    )(side, features)


def sums_kernel(d, pos_ref, table_ref, pat0_ref, pat1_ref, feat0_ref, feat1_ref, *rest):
    if not d:
        seed_ref, w_ref, bias_ref, even_ref, odd_ref, self_ref, *scratch = rest
        bias = jnp.where(pos_ref[4] == 0, bias_ref[...], 0.0)
        self_ref[...] = F32(seed_ref[...], w_ref[...], (((1,), (0,)), ((), ()))) + bias
    else:
        even_ref, odd_ref, *scratch = rest
    tiles, accs, pops, pats, feats, done = scratch[0:2], scratch[2:4], scratch[4:7], scratch[7:9], scratch[9:11], scratch[11]
    blocks = pats[0].shape[0]
    first = lax.rem(pos_ref[0] + d, NX) * blocks
    group = pl.ds(first, blocks)
    half = pl.ds(pl.multiple_of(pos_ref[2] * HALF, HALF), HALF)
    copies = [
        pltpu.make_async_copy(pat0_ref.at[group], pats[0], done.at[0]),
        pltpu.make_async_copy(pat1_ref.at[group], pats[1], done.at[1]),
        pltpu.make_async_copy(feat0_ref.at[:, half], feats[0], done.at[2]),
        pltpu.make_async_copy(feat1_ref, feats[1], done.at[3]),
    ]
    for copy in copies:
        copy.start()
    copies[0].wait()
    copies[1].wait()
    slots = [(side, slot) for side in range(2) for slot in range(FAN)]
    put = put_coded if d else put_plain

    def unpack(i, tile_ref, pop_ref):
        shifts = lax.broadcasted_iota(jnp.int32, (8, 16, BLK), 1)
        total = jnp.zeros((8, BLK), jnp.int32)
        for j, (side, slot) in enumerate(slots):
            live = table_ref[side * 32 + first + i]
            words = pats[side][i, slot] * (slot < live).astype(jnp.int32)
            total += lax.population_count(words)
            bits = (jnp.broadcast_to(words[:, None, :], (8, 16, BLK)) >> shifts) & 1
            tile_ref[pl.ds(j * BLK, BLK), :] = bits.reshape(BLK, BLK).astype(jnp.float32).astype(jnp.bfloat16)
        pop_ref[...] = total

    def multiply(i, tile_ref, acc_ref):
        picked = []
        for side, slot in slots:
            source = table_ref[64 + (side * 32 + first + i) * FAN + slot]
            picked.append(feats[side][pl.ds(pl.multiple_of(source * BLK, BLK), BLK), :])
        acc_ref[...] = F32(tile_ref[...], jnp.concatenate(picked, axis=0), (((0,), (0,)), ((), ()))).T

    def finish(i, acc_ref, pop_ref):
        count = jnp.sum(pop_ref[...], axis=0, keepdims=True).astype(jnp.float32)
        put((even_ref, odd_ref)[i % 2].at[i // 2], acc_ref[...], count)

    for step in range(blocks + 2):
        if step < blocks:
            unpack(step, tiles[step % 2], pops[step % 3])
        if step == 0:
            copies[2].wait()
            copies[3].wait()
        if 0 <= step - 1 < blocks:
            multiply(step - 1, tiles[(step - 1) % 2], accs[(step - 1) % 2])
        if 0 <= step - 2 < blocks:
            finish(step - 2, accs[(step - 2) % 2], pops[(step - 2) % 3])


def sums(d, pos, table, pat0, pat1, feat0, feat1, *more):
    blocks = 2 * NZ
    rows, kind = (HALF + 16, jnp.int16) if d else (HALF + 8, jnp.float32)
    nodes = feat0.shape[0]
    return pl.pallas_call(
        functools.partial(sums_kernel, d),
        out_shape=[jax.ShapeDtypeStruct((NZ, rows, BLK), kind)] * 2
        + [jax.ShapeDtypeStruct((BLK, weights.shape[1]), jnp.float32) for weights in more[1:2]],
        in_specs=[SMEM] * 2 + [pl.BlockSpec(memory_space=pl.ANY)] * 4 + [VMEM] * len(more),
        out_specs=[VMEM] * (3 if d == 0 else 2),
        scratch_shapes=[pltpu.VMEM((2 * FAN * BLK, BLK), jnp.bfloat16)] * 2
        + [pltpu.VMEM((HALF, BLK), jnp.float32)] * 2
        + [pltpu.VMEM((8, BLK), jnp.int32)] * 3
        + [pltpu.VMEM((blocks,) + pat0.shape[1:], jnp.int32)] * 2
        + [pltpu.VMEM((nodes, HALF), jnp.bfloat16)] * 2
        + [pltpu.SemaphoreType.DMA((4,))],
        compiler_params=ALONE,
        cost_estimate=pl.CostEstimate(flops=2_000_000_000, bytes_accessed=3_000_000, transcendentals=0),
        name="sums",
    )(pos, table, pat0, pat1, feat0, feat1, *more)


def call(kernel, name, outs, count, scratch=(), waits=0, params=PARAMS):
    return pl.pallas_call(
        kernel,
        out_shape=outs,
        in_specs=[SMEM] + [VMEM] * count + [pl.BlockSpec(memory_space=pl.ANY)] * waits,
        out_specs=[VMEM] * len(outs),
        scratch_shapes=list(scratch),
        compiler_params=params,
        name=name,
    )


def shaped(*dims):
    return jax.ShapeDtypeStruct(dims[:-1], dims[-1])


SUM_CODED = shaped(2, HALF + 16, BLK, jnp.int16)
SUM_PLAIN = shaped(2, HALF + 8, BLK, jnp.float32)
CODED = shaped(HALF + 16, BLK, jnp.int16)
PLAIN = shaped(HALF + 8, BLK, jnp.float32)
HALF16 = shaped(HALF, BLK, jnp.bfloat16)


def merge_x_kernel(pos_ref, *rest):
    for d, out_ref in enumerate(rest[-4:]):
        for c in range(2):
            index = lax.rem(pos_ref[1] + d, NZ)
            total, count = gathered((rest[6 + c].at[index],), [ref.at[index] for ref in rest[c:6:2]])
            (put_coded if d else put_plain)(out_ref.at[c], total, count)


def merge_z_kernel(pos_ref, r1_ref, r2_ref, r3_ref, own_ref, *rest):
    mine_ref, give_ref, rest_ref = rest[-3:]
    core = pos_ref[2]
    for out_ref, index in ((mine_ref, core), (give_ref, 1 - core)):
        total, count = gathered((own_ref.at[index],), [ref.at[index] for ref in (r1_ref, r2_ref, r3_ref)])
        out_ref[pl.ds(0, HALF), :] = (total / jnp.sqrt(1.0 + count)).astype(jnp.bfloat16)
    for block in range(HALF // 32):
        keep = pl.ds(pl.multiple_of(block * 32 + core * 16, 16), 16)
        give = pl.ds(pl.multiple_of(block * 32 + 16 - core * 16, 16), 16)
        give_ref[pl.ds(HALF + block * 16, 16), :] = mine_ref[give, :]
        rest_ref[pl.ds(block * 16, 16), :] = give_ref[keep, :]


def pre_kernel(
    pos_ref, mine_ref, got_ref, rest_ref, w_ref, self_ref, own_ref, o1_ref, o2_ref, o3_ref, agg0_ref, agg1_ref, agg, acc
):
    core = pos_ref[2]
    agg[pl.ds(pl.multiple_of(core * HALF, HALF), HALF), :] = mine_ref[...]
    agg[pl.ds(pl.multiple_of((1 - core) * HALF, HALF), HALF), :] = got_ref[pl.ds(0, HALF), :]
    acc[...] = (self_ref[...] + F32(agg[...], w_ref[...], (((0,), (0,)), ((), ())))).T
    for d, out_ref in enumerate((own_ref, o1_ref, o2_ref, o3_ref)):
        terms = acc[pl.ds(pl.multiple_of(lax.rem(pos_ref[3] + d, NY) * HALF, HALF), HALF), :]
        (put_coded if d else put_plain)(out_ref, terms, jnp.zeros((1, BLK), jnp.float32))
    for block in range(WIDE // 32):
        rows = pl.ds(pl.multiple_of(block * 32 + core * 16, 16), 16)
        agg0_ref[pl.ds(block * 16, 16), :] = agg[rows, :]
    agg1_ref[pl.ds(pl.multiple_of(core * BLK, BLK), BLK), :] = rest_ref[...]
    agg1_ref[pl.ds(pl.multiple_of((1 - core) * BLK, BLK), BLK), :] = got_ref[pl.ds(HALF, BLK), :]


def merge_y_kernel(pos_ref, r1_ref, r2_ref, r3_ref, own_ref, out_ref):
    total, count = gathered((own_ref,), (r1_ref, r2_ref, r3_ref))
    put_coded(out_ref, total, count)


def hidden_kernel(pos_ref, own_ref, far_ref, out_ref):
    out_ref[...] = jnp.maximum(decode(own_ref)[0] + decode(far_ref)[0], 0.0).astype(jnp.bfloat16)


def grads_kernel(
    pos_ref, a0_ref, a1_ref, a2_ref, a3_ref, b0_ref, b1_ref, b2_ref, b3_ref, og0_ref, og1_ref,
    agg0_ref, agg1_ref, seed0_ref, seed1_ref,
    hidden_ref, *rest,
):
    self_refs, neigh_refs = rest[:4], rest[4:8]
    rows, self_acc, neigh_acc, bias = rest[8:]
    x, y = pos_ref[0], pos_ref[3]
    zero = jnp.zeros((BLK, HALF), jnp.bfloat16)
    for d in range(NY):
        place = pl.ds(pl.multiple_of(lax.rem(y + NY - d, NY) * HALF, HALF), HALF)
        for side, (refs, og_ref) in enumerate(
            (((a0_ref, a1_ref, a2_ref, a3_ref), og0_ref), ((b0_ref, b1_ref, b2_ref, b3_ref), og1_ref))
        ):
            value = refs[d][...].T
            if side == 0:
                hidden_ref[:, place] = value
            rows[pl.ds(side * BLK, BLK), place] = jnp.where(value > 0, og_ref[:, place], zero)
    hid = rows.shape[1]
    contract = (((1,), (0,)), ((), ()))
    self_acc[...] = F32(jnp.concatenate([seed0_ref[...], seed1_ref[...]], axis=1), rows[...], contract)
    neigh_acc[...] = F32(jnp.concatenate([agg0_ref[...], agg1_ref[...]], axis=1), rows[...], contract)
    total = F32(jnp.ones((8, 2 * BLK), jnp.bfloat16), rows[...], contract)[0:1]
    for part in range(hid // BLK):
        bias[pl.ds(part, 1), :] = total[:, part * BLK:(part + 1) * BLK]
    row = lax.broadcasted_iota(jnp.int32, (16, BLK), 0)
    for d in range(NX):
        to = lax.rem(x + d, NX)
        take = pl.ds(pl.multiple_of(to * 64, 64), 64)
        out_ref = self_refs[d]
        out_ref[:, pl.ds(0, hid)] = self_acc[take, :].astype(out_ref.dtype)
        neigh_refs[d][...] = neigh_acc[take, :].astype(out_ref.dtype)
        left, right = bias[pl.ds(to * 2, 1), :], bias[pl.ds(to * 2 + 1, 1), :]
        left_top = left.astype(jnp.bfloat16).astype(jnp.float32)
        right_top = right.astype(jnp.bfloat16).astype(jnp.float32)
        mark = jnp.where(row == 0, left_top, jnp.where(row == 1, right_top, 0.0))
        mark = jnp.where(row == 2, left - left_top, jnp.where(row == 3, right - right_top, mark))
        out_ref[pl.ds(0, 16), pl.ds(hid, BLK)] = mark.astype(out_ref.dtype)
        out_ref[pl.ds(16, 48), pl.ds(hid, BLK)] = jnp.zeros((48, BLK), out_ref.dtype)


def fold_kernel(pos_ref, r1_ref, r2_ref, r3_ref, own_ref, kept_ref, o1_ref, o2_ref, o3_ref, total):
    total[...] = own_ref[...] + sum(ref[...].astype(jnp.float32) for ref in (r1_ref, r2_ref, r3_ref))
    for d, out_ref in enumerate((kept_ref, o1_ref, o2_ref, o3_ref)):
        take = pl.ds(pl.multiple_of(lax.rem(pos_ref[1] + d, NZ) * 16, 16), 16)
        out_ref[...] = total[take, :].astype(out_ref.dtype)


def fold_x_kernel(pos_ref, r1_ref, r2_ref, r3_ref, own_ref, kept_ref, o1_ref, o2_ref, o3_ref, total, bias):
    hid = total.shape[1]
    body, marks = pl.ds(0, hid), pl.ds(hid, BLK)
    refs = (r1_ref, r2_ref, r3_ref)
    total[...] = own_ref[:, body] + sum(ref[:, body].astype(jnp.float32) for ref in refs)
    top = pl.ds(0, 16)
    mark = own_ref[top, marks] + sum(ref[top, marks].astype(jnp.float32) for ref in refs)
    bias[pl.ds(0, 1), :] = mark[0:1] + mark[2:3]
    bias[pl.ds(1, 1), :] = mark[1:2] + mark[3:4]
    row = lax.broadcasted_iota(jnp.int32, (16, BLK), 0)
    for d, out_ref in enumerate((kept_ref, o1_ref, o2_ref, o3_ref)):
        to = lax.rem(pos_ref[1] + d, NZ)
        take = pl.ds(pl.multiple_of(to * 16, 16), 16)
        out_ref[:, body] = total[take, :].astype(out_ref.dtype)
        line = bias[pl.ds(to // 2, 1), :]
        high = line.astype(jnp.bfloat16).astype(jnp.float32)
        mark = jnp.where(row == 0, high, jnp.where(row == 1, line - high, 0.0))
        out_ref[top, marks] = mark.astype(out_ref.dtype)


def last_kernel(
    pos_ref, r1_ref, r2_ref, r3_ref, own_ref, n1_ref, n2_ref, n3_ref, n_ref, self_ref, neigh_ref, bias_ref
):
    hid = self_ref.shape[1]
    body, marks = pl.ds(0, hid), pl.ds(hid, BLK)
    refs = (r1_ref, r2_ref, r3_ref)
    self_ref[...] = own_ref[:, body] + sum(ref[:, body].astype(jnp.float32) for ref in refs)
    neigh_ref[...] = n_ref[...] + sum(ref[...].astype(jnp.float32) for ref in (n1_ref, n2_ref, n3_ref))
    mark = own_ref[:, marks] + sum(ref[:, marks].astype(jnp.float32) for ref in refs)
    line = mark[0:1] + mark[1:2]
    for place in range(BLK // 32):
        @pl.when(lax.rem(pos_ref[1], 2) * 2 + pos_ref[2] == place)
        def _():
            bias_ref[...] = line[:, place * 32:place * 32 + 32]


def body(features, seed_feats, patterns, sources, counts, w_self, w_neigh, bias_term, out_grad):
    node = lax.axis_index("node")
    feat = lax.axis_index("feat")
    x, z, core = node // (NZ * 2), (node // 2) % NZ, node % 2
    y = feat % NY
    pos = jnp.stack([x, z, core, y, feat]).astype(jnp.int32)
    hid = w_self.shape[1]
    swap = lambda value: lax.ppermute(value, "node", SWAP_CORE)

    packed = patterns.transpose(0, 1, 3, 2)
    table = jnp.concatenate([counts, sources.reshape(-1)])
    packed_other, table_other = swap(packed), swap(table)
    other = swap(half_columns((1 - core)[None].astype(jnp.int32), features))
    lists = counts.shape[0]
    table = jnp.concatenate([table[:lists], table_other[:lists], table[lists:], table_other[lists:]])

    made = {}
    for d in (2, 1, 3, 0):
        more = () if d else (seed_feats, w_self, bias_term[None])
        made[d] = sums(d, pos, table, packed, packed_other, features, other, *more)
    far = [lax.ppermute(part, "node", shift_x(d)) for d in (2, 1, 3) for part in made[d]]

    *own, self_term = made[0]
    seed_feats, out_grad, own = lax.optimization_barrier((seed_feats, out_grad, own))
    turned = seed_feats.T.reshape(WIDE // 32, 2, 16, BLK)
    pick = lambda c: lax.dynamic_index_in_dim(turned, c, 1, keepdims=False).reshape(HALF, BLK)
    seed_mine, seed_other = pick(core), swap(pick(1 - core))
    og_other = swap(out_grad)

    own, *coded = call(merge_x_kernel, "merge_x", [SUM_PLAIN] + [SUM_CODED] * 3, 8, params=ALONE)(
        pos, *far, *own
    )
    arrived = [lax.ppermute(coded[d - 1], "node", shift_z(d)) for d in (2, 1, 3)]
    mine, give, rest = call(
        merge_z_kernel, "merge_z", [HALF16, shaped(HALF + BLK, BLK, jnp.bfloat16), shaped(BLK, BLK, jnp.bfloat16)], 4
    )(pos, *arrived, own)

    *coded, agg_mine, agg_other = call(
        pre_kernel, "pre_terms", [PLAIN] + [CODED] * 3 + [HALF16] * 2, 5,
        [pltpu.VMEM((WIDE, BLK), jnp.bfloat16), pltpu.VMEM((hid, BLK), jnp.float32)],
    )(pos, mine, swap(give), rest, w_neigh, self_term)
    own, *coded = coded
    received = [lax.ppermute(coded[d - 1], "feat", shift_y(d)) for d in (2, 1, 3)]
    (coded,) = call(merge_y_kernel, "merge_y", [CODED], 4)(pos, *received, own)
    far = lax.ppermute(coded, "feat", SWAP_FAR)
    (own,) = call(hidden_kernel, "hidden", [HALF16], 2)(pos, coded, far)
    chunks = [own] + [lax.ppermute(own, "feat", shift_y(d)) for d in (1, 2, 3)]
    chunks_other = [swap(chunk) for chunk in chunks]

    wide = hid + BLK
    scratch = [
        pltpu.VMEM((2 * BLK, hid), jnp.bfloat16),
        pltpu.VMEM((HALF, hid), jnp.float32),
        pltpu.VMEM((HALF, hid), jnp.float32),
        pltpu.VMEM((8, BLK), jnp.float32),
    ]
    cut = lambda rows, cols: [shaped(rows, cols, jnp.float32)] + [shaped(rows, cols, jnp.bfloat16)] * 3
    hidden, *parts = call(
        grads_kernel, "grads", [shaped(BLK, hid, jnp.bfloat16)] + cut(64, wide) + cut(64, hid), 14, scratch
    )(pos, *chunks, *chunks_other, out_grad, og_other, agg_mine, agg_other, seed_mine, seed_other)
    chains = []
    for chain, cols in ((parts[:4], wide), (parts[4:], hid)):
        chains.append([lax.ppermute(chain[d], "node", shift_x(d)) for d in (2, 1, 3)] + chain[:1])
    folded = [
        call(
            fold_x_kernel, "fold_self", cut(16, wide), 4,
            [pltpu.VMEM((64, hid), jnp.float32), pltpu.VMEM((8, BLK), jnp.float32)],
        )(pos, *chains[0]),
        call(fold_kernel, "fold_neigh", cut(16, hid), 4, [pltpu.VMEM((64, hid), jnp.float32)])(pos, *chains[1]),
    ]
    received = []
    for own, *chain in folded:
        received += [lax.ppermute(chain[d - 1], "node", shift_z(d)) for d in (2, 1, 3)] + [own]
    part = shaped(16, hid, jnp.float32)
    grad_self, grad_neigh, bias = call(last_kernel, "last", [part, part, shaped(1, 32, jnp.float32)], 8)(
        pos, *received
    )
    return (hidden, grad_self, grad_neigh, bias[0])


def solution(mesh):
    return jax.shard_map(
        body,
        mesh=mesh,
        in_specs=(
            P("node", "feat"),
            P("node", "feat"),
            P("node", None, None, None),
            P("node", None),
            P("node"),
            P("feat", None),
            P("feat", None),
            P(),
            P("node", None),
        ),
        out_specs=(
            P("node", None),
            P(("feat", "node"), None),
            P(("feat", "node"), None),
            P("node"),
        ),
        check_vma=False,
    )
```

```python
import functools

import jax
import jax.numpy as jnp
from jax import lax
from jax.experimental import pallas as pl
from jax.experimental.pallas import tpu as pltpu
from jax.sharding import PartitionSpec as P

BLK = 128
HALF = 256
FAN = 8
TOP = 32700.0
NX, NZ, NY = 4, 4, 4
WIDE = 512
VMEM = pl.BlockSpec(memory_space=pltpu.VMEM)
SMEM = pl.BlockSpec(memory_space=pltpu.SMEM)
PARAMS = pltpu.CompilerParams(vmem_limit_bytes=40 * 1024 * 1024)
ALONE = pltpu.CompilerParams(vmem_limit_bytes=63 * 1024 * 1024)
F32 = functools.partial(lax.dot_general, preferred_element_type=jnp.float32)


def node_of(x, z, c):
    return x * (NZ * 2) + z * 2 + c


NODES = [(x, z, c) for x in range(NX) for z in range(NZ) for c in range(2)]
SWAP_CORE = [(n, n ^ 1) for n in range(NX * NZ * 2)]
SWAP_FAR = [(f, f ^ 4) for f in range(8)]


def shift_x(d):
    return [(node_of(x, z, c), node_of((x + d) % NX, z, c)) for x, z, c in NODES]


def shift_z(d):
    return [(node_of(x, z, c), node_of(x, (z + d) % NZ, c)) for x, z, c in NODES]


def shift_y(d):
    return [(h * 4 + y, h * 4 + (y + d) % NY) for h in range(2) for y in range(NY)]


def step_of(mantissa, exponent):
    return mantissa * jnp.exp2(exponent)


def encode(sums, count):
    top = jnp.maximum(jnp.max(jnp.abs(sums), axis=0, keepdims=True), 1e-25) * (1.0 / TOP)
    exponent = jnp.floor(jnp.log2(top)) - 13.0
    mantissa = jnp.ceil(top * jnp.exp2(-exponent))
    coded = jnp.round(sums * (1.0 / step_of(mantissa, exponent))).astype(jnp.int32).astype(jnp.int16)
    row = lax.broadcasted_iota(jnp.int32, (16, BLK), 0)
    tail = jnp.where(row == 0, count, jnp.where(row == 1, exponent, jnp.where(row == 2, mantissa, 0.0)))
    return coded, tail.astype(jnp.int32).astype(jnp.int16)


def put_coded(ref, sums, count):
    rows = sums.shape[0]
    coded, tail = encode(sums, count)
    ref[pl.ds(0, rows), :] = coded
    ref[pl.ds(rows, 16), :] = tail


def put_plain(ref, sums, count):
    rows = sums.shape[0]
    ref[pl.ds(0, rows), :] = sums
    ref[pl.ds(rows, 8), :] = jnp.broadcast_to(count, (8, BLK))


def plain(ref):
    rows = ref.shape[0] - 8
    return ref[pl.ds(0, rows), :], ref[pl.ds(rows, 8), :][0:1]


def decode(ref):
    rows = ref.shape[0] - 16
    tail = ref[pl.ds(rows, 16), :].astype(jnp.int32).astype(jnp.float32)
    values = ref[pl.ds(0, rows), :].astype(jnp.int32).astype(jnp.float32)
    return values * step_of(tail[2:3], tail[1:2]), tail[0:1]


def gathered(plain_refs, coded_refs):
    pairs = [plain(ref) for ref in plain_refs] + [decode(ref) for ref in coded_refs]
    return sum(pair[0] for pair in pairs), sum(pair[1] for pair in pairs)


def half_kernel(side_ref, features_ref, out_ref, held, came, went):
    parts = came.shape[0]
    step = held.shape[0] // parts
    cols = pl.ds(pl.multiple_of(side_ref[0] * HALF, HALF), HALF)
    take, give = [], []
    for part in range(parts):
        rows = pl.ds(part * step, step)
        take.append(pltpu.make_async_copy(features_ref.at[rows, cols], held.at[rows, :], came.at[part]))
        give.append(pltpu.make_async_copy(held.at[rows, :], out_ref.at[rows, :], went.at[part]))
    for copy in take:
        copy.start()
    for part in range(parts):
        take[part].wait()
        give[part].start()
    for copy in give:
        copy.wait()


def half_columns(side, features):
    nodes = features.shape[0]
    return pl.pallas_call(
        half_kernel,
        out_shape=jax.ShapeDtypeStruct((nodes, HALF), features.dtype),
        in_specs=[SMEM, pl.BlockSpec(memory_space=pl.ANY)],
        out_specs=pl.BlockSpec(memory_space=pl.ANY),
        scratch_shapes=[pltpu.VMEM((nodes, HALF), features.dtype)] + [pltpu.SemaphoreType.DMA((8,))] * 2,
        compiler_params=ALONE,
        name="half_columns",
    )(side, features)


def sums_kernel(d, pos_ref, table_ref, pat0_ref, pat1_ref, feat0_ref, feat1_ref, *rest):
    if not d:
        seed_ref, w_ref, bias_ref, even_ref, odd_ref, self_ref, *scratch = rest
        bias = jnp.where(pos_ref[4] == 0, bias_ref[...], 0.0)
        self_ref[...] = F32(seed_ref[...], w_ref[...], (((1,), (0,)), ((), ()))) + bias
    else:
        even_ref, odd_ref, *scratch = rest
    tiles, accs, pops, pats, feats, done = scratch[0:2], scratch[2:4], scratch[4:7], scratch[7:9], scratch[9:11], scratch[11]
    blocks = pats[0].shape[0]
    first = lax.rem(pos_ref[0] + d, NX) * blocks
    group = pl.ds(first, blocks)
    half = pl.ds(pl.multiple_of(pos_ref[2] * HALF, HALF), HALF)
    copies = [
        pltpu.make_async_copy(pat0_ref.at[group], pats[0], done.at[0]),
        pltpu.make_async_copy(pat1_ref.at[group], pats[1], done.at[1]),
        pltpu.make_async_copy(feat0_ref.at[:, half], feats[0], done.at[2]),
        pltpu.make_async_copy(feat1_ref, feats[1], done.at[3]),
    ]
    for copy in copies:
        copy.start()
    copies[0].wait()
    copies[1].wait()
    slots = [(side, slot) for side in range(2) for slot in range(FAN)]
    put = put_coded if d else put_plain

    def unpack(i, tile_ref, pop_ref):
        shifts = lax.broadcasted_iota(jnp.int32, (8, 16, BLK), 1)
        total = jnp.zeros((8, BLK), jnp.int32)
        for j, (side, slot) in enumerate(slots):
            live = table_ref[side * 32 + first + i]
            words = pats[side][i, slot] * (slot < live).astype(jnp.int32)
            total += lax.population_count(words)
            bits = (jnp.broadcast_to(words[:, None, :], (8, 16, BLK)) >> shifts) & 1
            tile_ref[pl.ds(j * BLK, BLK), :] = bits.reshape(BLK, BLK).astype(jnp.float32).astype(jnp.bfloat16)
        pop_ref[...] = total

    def multiply(i, tile_ref, acc_ref):
        picked = []
        for side, slot in slots:
            source = table_ref[64 + (side * 32 + first + i) * FAN + slot]
            picked.append(feats[side][pl.ds(pl.multiple_of(source * BLK, BLK), BLK), :])
        acc_ref[...] = F32(tile_ref[...], jnp.concatenate(picked, axis=0), (((0,), (0,)), ((), ()))).T

    def finish(i, acc_ref, pop_ref):
        count = jnp.sum(pop_ref[...], axis=0, keepdims=True).astype(jnp.float32)
        put((even_ref, odd_ref)[i % 2].at[i // 2], acc_ref[...], count)

    for step in range(blocks + 2):
        if step < blocks:
            unpack(step, tiles[step % 2], pops[step % 3])
        if step == 0:
            copies[2].wait()
            copies[3].wait()
        if 0 <= step - 1 < blocks:
            multiply(step - 1, tiles[(step - 1) % 2], accs[(step - 1) % 2])
        if 0 <= step - 2 < blocks:
            finish(step - 2, accs[(step - 2) % 2], pops[(step - 2) % 3])


def sums(d, pos, table, pat0, pat1, feat0, feat1, *more):
    blocks = 2 * NZ
    rows, kind = (HALF + 16, jnp.int16) if d else (HALF + 8, jnp.float32)
    nodes = feat0.shape[0]
    return pl.pallas_call(
        functools.partial(sums_kernel, d),
        out_shape=[jax.ShapeDtypeStruct((NZ, rows, BLK), kind)] * 2
        + [jax.ShapeDtypeStruct((BLK, weights.shape[1]), jnp.float32) for weights in more[1:2]],
        in_specs=[SMEM] * 2 + [pl.BlockSpec(memory_space=pl.ANY)] * 4 + [VMEM] * len(more),
        out_specs=[VMEM] * (3 if more else 2),
        scratch_shapes=[pltpu.VMEM((2 * FAN * BLK, BLK), jnp.bfloat16)] * 2
        + [pltpu.VMEM((HALF, BLK), jnp.float32)] * 2
        + [pltpu.VMEM((8, BLK), jnp.int32)] * 3
        + [pltpu.VMEM((blocks,) + pat0.shape[1:], jnp.int32)] * 2
        + [pltpu.VMEM((nodes, HALF), jnp.bfloat16)] * 2
        + [pltpu.SemaphoreType.DMA((4,))],
        compiler_params=ALONE,
        cost_estimate=pl.CostEstimate(flops=2_000_000_000, bytes_accessed=3_000_000, transcendentals=0),
        name="sums",
    )(pos, table, pat0, pat1, feat0, feat1, *more)


def call(kernel, name, outs, count, scratch=(), waits=0, params=PARAMS):
    return pl.pallas_call(
        kernel,
        out_shape=outs,
        in_specs=[SMEM] + [VMEM] * count + [pl.BlockSpec(memory_space=pl.ANY)] * waits,
        out_specs=[VMEM] * len(outs),
        scratch_shapes=list(scratch),
        compiler_params=params,
        name=name,
    )


def shaped(*dims):
    return jax.ShapeDtypeStruct(dims[:-1], dims[-1])


SUM_CODED = shaped(2, HALF + 16, BLK, jnp.int16)
SUM_PLAIN = shaped(2, HALF + 8, BLK, jnp.float32)
CODED = shaped(HALF + 16, BLK, jnp.int16)
PLAIN = shaped(HALF + 8, BLK, jnp.float32)
HALF16 = shaped(HALF, BLK, jnp.bfloat16)


def merge_x_kernel(pos_ref, *rest):
    for d, out_ref in enumerate(rest[-4:]):
        for c in range(2):
            index = lax.rem(pos_ref[1] + d, NZ)
            total, count = gathered((rest[6 + c].at[index],), [ref.at[index] for ref in rest[c:6:2]])
            (put_coded if d else put_plain)(out_ref.at[c], total, count)


def merge_z_kernel(pos_ref, r1_ref, r2_ref, r3_ref, own_ref, *rest):
    mine_ref, give_ref, rest_ref = rest[-3:]
    core = pos_ref[2]
    for out_ref, index in ((mine_ref, core), (give_ref, 1 - core)):
        total, count = gathered((own_ref.at[index],), [ref.at[index] for ref in (r1_ref, r2_ref, r3_ref)])
        out_ref[pl.ds(0, HALF), :] = (total / jnp.sqrt(1.0 + count)).astype(jnp.bfloat16)
    for block in range(HALF // 32):
        keep = pl.ds(pl.multiple_of(block * 32 + core * 16, 16), 16)
        give = pl.ds(pl.multiple_of(block * 32 + 16 - core * 16, 16), 16)
        give_ref[pl.ds(HALF + block * 16, 16), :] = mine_ref[give, :]
        rest_ref[pl.ds(block * 16, 16), :] = give_ref[keep, :]


def pre_kernel(
    pos_ref, mine_ref, got_ref, rest_ref, w_ref, self_ref, own_ref, o1_ref, o2_ref, o3_ref, agg0_ref, agg1_ref, agg, acc
):
    core = pos_ref[2]
    agg[pl.ds(pl.multiple_of(core * HALF, HALF), HALF), :] = mine_ref[...]
    agg[pl.ds(pl.multiple_of((1 - core) * HALF, HALF), HALF), :] = got_ref[pl.ds(0, HALF), :]
    acc[...] = (self_ref[...] + F32(agg[...], w_ref[...], (((0,), (0,)), ((), ())))).T
    for d, out_ref in enumerate((own_ref, o1_ref, o2_ref, o3_ref)):
        terms = acc[pl.ds(pl.multiple_of(lax.rem(pos_ref[3] + d, NY) * HALF, HALF), HALF), :]
        (put_coded if d else put_plain)(out_ref, terms, jnp.zeros((1, BLK), jnp.float32))
    for block in range(WIDE // 32):
        rows = pl.ds(pl.multiple_of(block * 32 + core * 16, 16), 16)
        agg0_ref[pl.ds(block * 16, 16), :] = agg[rows, :]
    agg1_ref[pl.ds(pl.multiple_of(core * BLK, BLK), BLK), :] = rest_ref[...]
    agg1_ref[pl.ds(pl.multiple_of((1 - core) * BLK, BLK), BLK), :] = got_ref[pl.ds(HALF, BLK), :]


def merge_y_kernel(pos_ref, r1_ref, r2_ref, r3_ref, own_ref, out_ref):
    total, count = gathered((own_ref,), (r1_ref, r2_ref, r3_ref))
    put_coded(out_ref, total, count)


def hidden_kernel(pos_ref, own_ref, far_ref, out_ref):
    out_ref[...] = jnp.maximum(decode(own_ref)[0] + decode(far_ref)[0], 0.0).astype(jnp.bfloat16)


def grads_kernel(
    pos_ref, a0_ref, a1_ref, a2_ref, a3_ref, b0_ref, b1_ref, b2_ref, b3_ref, og0_ref, og1_ref,
    agg0_ref, agg1_ref, seed0_ref, seed1_ref,
    hidden_ref, own_ref, o1_ref, o2_ref, o3_ref, rows, self_acc, neigh_acc, bias,
):
    x, y = pos_ref[0], pos_ref[3]
    zero = jnp.zeros((BLK, HALF), jnp.bfloat16)
    for d in range(NY):
        place = pl.ds(pl.multiple_of(lax.rem(y + NY - d, NY) * HALF, HALF), HALF)
        for side, (refs, og_ref) in enumerate(
            (((a0_ref, a1_ref, a2_ref, a3_ref), og0_ref), ((b0_ref, b1_ref, b2_ref, b3_ref), og1_ref))
        ):
            value = refs[d][...].T
            if side == 0:
                hidden_ref[:, place] = value
            rows[pl.ds(side * BLK, BLK), place] = jnp.where(value > 0, og_ref[:, place], zero)
    hid = rows.shape[1]
    contract = (((1,), (0,)), ((), ()))
    self_acc[...] = F32(jnp.concatenate([seed0_ref[...], seed1_ref[...]], axis=1), rows[...], contract)
    neigh_acc[...] = F32(jnp.concatenate([agg0_ref[...], agg1_ref[...]], axis=1), rows[...], contract)
    total = F32(jnp.ones((8, 2 * BLK), jnp.bfloat16), rows[...], contract)[0:1]
    for part in range(hid // BLK):
        bias[pl.ds(part, 1), :] = total[:, part * BLK:(part + 1) * BLK]
    row = lax.broadcasted_iota(jnp.int32, (16, BLK), 0)
    for d, out_ref in enumerate((own_ref, o1_ref, o2_ref, o3_ref)):
        to = lax.rem(x + d, NX)
        take = pl.ds(pl.multiple_of(to * 64, 64), 64)
        out_ref[pl.ds(0, 64), pl.ds(0, hid)] = self_acc[take, :].astype(out_ref.dtype)
        out_ref[pl.ds(64, 64), pl.ds(0, hid)] = neigh_acc[take, :].astype(out_ref.dtype)
        left, right = bias[pl.ds(to * 2, 1), :], bias[pl.ds(to * 2 + 1, 1), :]
        left_top = left.astype(jnp.bfloat16).astype(jnp.float32)
        right_top = right.astype(jnp.bfloat16).astype(jnp.float32)
        mark = jnp.where(row == 0, left_top, jnp.where(row == 1, right_top, 0.0))
        mark = jnp.where(row == 2, left - left_top, jnp.where(row == 3, right - right_top, mark))
        out_ref[pl.ds(0, 16), pl.ds(hid, BLK)] = mark.astype(out_ref.dtype)
        out_ref[pl.ds(16, 112), pl.ds(hid, BLK)] = jnp.zeros((112, BLK), out_ref.dtype)


def fold_x_kernel(pos_ref, r1_ref, r2_ref, r3_ref, own_ref, kept_ref, o1_ref, o2_ref, o3_ref, total, bias):
    hid = total.shape[1]
    body, marks = pl.ds(0, hid), pl.ds(hid, BLK)
    refs = (r1_ref, r2_ref, r3_ref)
    total[...] = own_ref[:, body] + sum(ref[:, body].astype(jnp.float32) for ref in refs)
    top = pl.ds(0, 16)
    mark = own_ref[top, marks] + sum(ref[top, marks].astype(jnp.float32) for ref in refs)
    bias[pl.ds(0, 1), :] = mark[0:1] + mark[2:3]
    bias[pl.ds(1, 1), :] = mark[1:2] + mark[3:4]
    row = lax.broadcasted_iota(jnp.int32, (16, BLK), 0)
    for d, out_ref in enumerate((kept_ref, o1_ref, o2_ref, o3_ref)):
        to = lax.rem(pos_ref[1] + d, NZ)
        for kind in range(2):
            take = pl.ds(pl.multiple_of(kind * 64 + to * 16, 16), 16)
            out_ref[pl.ds(kind * 16, 16), body] = total[take, :].astype(out_ref.dtype)
        line = bias[pl.ds(to // 2, 1), :]
        high = line.astype(jnp.bfloat16).astype(jnp.float32)
        mark = jnp.where(row == 0, high, jnp.where(row == 1, line - high, 0.0))
        out_ref[top, marks] = mark.astype(out_ref.dtype)
        out_ref[pl.ds(16, 16), marks] = jnp.zeros((16, BLK), out_ref.dtype)


def last_kernel(pos_ref, r1_ref, r2_ref, r3_ref, own_ref, self_ref, neigh_ref, bias_ref):
    hid = self_ref.shape[1]
    body, marks = pl.ds(0, hid), pl.ds(hid, BLK)
    refs = (r1_ref, r2_ref, r3_ref)
    total = own_ref[:, body] + sum(ref[:, body].astype(jnp.float32) for ref in refs)
    top = pl.ds(0, 16)
    mark = own_ref[top, marks] + sum(ref[top, marks].astype(jnp.float32) for ref in refs)
    self_ref[...] = total[:16]
    neigh_ref[...] = total[16:]
    line = mark[0:1] + mark[1:2]
    for place in range(BLK // 32):
        @pl.when(lax.rem(pos_ref[1], 2) * 2 + pos_ref[2] == place)
        def _():
            bias_ref[...] = line[:, place * 32:place * 32 + 32]


def body(features, seed_feats, patterns, sources, counts, w_self, w_neigh, bias_term, out_grad):
    node = lax.axis_index("node")
    feat = lax.axis_index("feat")
    x, z, core = node // (NZ * 2), (node // 2) % NZ, node % 2
    y = feat % NY
    pos = jnp.stack([x, z, core, y, feat]).astype(jnp.int32)
    hid = w_self.shape[1]
    swap = lambda value: lax.ppermute(value, "node", SWAP_CORE)

    packed = patterns.transpose(0, 1, 3, 2)
    table = jnp.concatenate([counts, sources.reshape(-1)])
    packed_other, table_other = swap(packed), swap(table)
    other = swap(half_columns((1 - core)[None].astype(jnp.int32), features))
    lists = counts.shape[0]
    table = jnp.concatenate([table[:lists], table_other[:lists], table[lists:], table_other[lists:]])

    made = {}
    for d in (2, 1, 3, 0):
        more = () if d else (seed_feats, w_self, bias_term[None])
        made[d] = sums(d, pos, table, packed, packed_other, features, other, *more)
    far = [lax.ppermute(part, "node", shift_x(d)) for d in (2, 1, 3) for part in made[d]]

    *own, self_term = made[0]
    seed_feats, out_grad, own = lax.optimization_barrier((seed_feats, out_grad, own))
    turned = seed_feats.T.reshape(WIDE // 32, 2, 16, BLK)
    pick = lambda c: lax.dynamic_index_in_dim(turned, c, 1, keepdims=False).reshape(HALF, BLK)
    seed_mine, seed_other = pick(core), swap(pick(1 - core))
    og_other = swap(out_grad)

    own, *coded = call(merge_x_kernel, "merge_x", [SUM_PLAIN] + [SUM_CODED] * 3, 8, params=ALONE)(
        pos, *far, *own
    )
    arrived = [lax.ppermute(coded[d - 1], "node", shift_z(d)) for d in (2, 1, 3)]
    mine, give, rest = call(
        merge_z_kernel, "merge_z", [HALF16, shaped(HALF + BLK, BLK, jnp.bfloat16), shaped(BLK, BLK, jnp.bfloat16)], 4, params=ALONE
    )(pos, *arrived, own)

    *coded, agg_mine, agg_other = call(
        pre_kernel, "pre_terms", [PLAIN] + [CODED] * 3 + [HALF16] * 2, 5,
        [pltpu.VMEM((WIDE, BLK), jnp.bfloat16), pltpu.VMEM((hid, BLK), jnp.float32)], params=ALONE,
    )(pos, mine, swap(give), rest, w_neigh, self_term)
    own, *coded = coded
    received = [lax.ppermute(coded[d - 1], "feat", shift_y(d)) for d in (2, 1, 3)]
    (coded,) = call(merge_y_kernel, "merge_y", [CODED], 4)(pos, *received, own)
    far = lax.ppermute(coded, "feat", SWAP_FAR)
    (own,) = call(hidden_kernel, "hidden", [HALF16], 2)(pos, coded, far)
    chunks = [own] + [lax.ppermute(own, "feat", shift_y(d)) for d in (1, 2, 3)]
    chunks_other = [swap(chunk) for chunk in chunks]

    wide = hid + BLK
    scratch = [
        pltpu.VMEM((2 * BLK, hid), jnp.bfloat16),
        pltpu.VMEM((HALF, hid), jnp.float32),
        pltpu.VMEM((HALF, hid), jnp.float32),
        pltpu.VMEM((8, BLK), jnp.float32),
    ]
    outs = [shaped(BLK, hid, jnp.bfloat16), shaped(BLK, wide, jnp.float32)] + [shaped(BLK, wide, jnp.bfloat16)] * 3
    hidden, own, *parts = call(grads_kernel, "grads", outs, 14, scratch)(
        pos, *chunks, *chunks_other, out_grad, og_other, agg_mine, agg_other, seed_mine, seed_other
    )
    received = [lax.ppermute(parts[d - 1], "node", shift_x(d)) for d in (2, 1, 3)]
    own, *parts = call(
        fold_x_kernel, "fold_x", [shaped(32, wide, jnp.float32)] + [shaped(32, wide, jnp.bfloat16)] * 3, 4,
        [pltpu.VMEM((BLK, hid), jnp.float32), pltpu.VMEM((8, BLK), jnp.float32)],
    )(pos, *received, own)
    received = [lax.ppermute(parts[d - 1], "node", shift_z(d)) for d in (2, 1, 3)]
    part = shaped(16, hid, jnp.float32)
    grad_self, grad_neigh, bias = call(last_kernel, "last", [part, part, shaped(1, 32, jnp.float32)], 4)(
        pos, *received, own
    )
    return (hidden, grad_self, grad_neigh, bias[0])


def solution(mesh):
    return jax.shard_map(
        body,
        mesh=mesh,
        in_specs=(
            P("node", "feat"),
            P("node", "feat"),
            P("node", None, None, None),
            P("node", None),
            P("node"),
            P("feat", None),
            P("feat", None),
            P(),
            P("node", None),
        ),
        out_specs=(
            P("node", None),
            P(("feat", "node"), None),
            P(("feat", "node"), None),
            P("node"),
        ),
        check_vma=False,
    )
```

```python
import functools

import jax
import jax.numpy as jnp
from jax import lax
from jax.experimental import pallas as pl
from jax.experimental.pallas import tpu as pltpu
from jax.sharding import PartitionSpec as P

BLK = 128
HALF = 256
FAN = 8
TOP = 32700.0
NX, NZ, NY = 4, 4, 4
WIDE = 512
VMEM = pl.BlockSpec(memory_space=pltpu.VMEM)
SMEM = pl.BlockSpec(memory_space=pltpu.SMEM)
PARAMS = pltpu.CompilerParams(vmem_limit_bytes=40 * 1024 * 1024)
ALONE = pltpu.CompilerParams(vmem_limit_bytes=63 * 1024 * 1024)
F32 = functools.partial(lax.dot_general, preferred_element_type=jnp.float32)


def node_of(x, z, c):
    return x * (NZ * 2) + z * 2 + c


NODES = [(x, z, c) for x in range(NX) for z in range(NZ) for c in range(2)]
SWAP_CORE = [(n, n ^ 1) for n in range(NX * NZ * 2)]
SWAP_FAR = [(f, f ^ 4) for f in range(8)]


def shift_x(d):
    return [(node_of(x, z, c), node_of((x + d) % NX, z, c)) for x, z, c in NODES]


def shift_z(d):
    return [(node_of(x, z, c), node_of(x, (z + d) % NZ, c)) for x, z, c in NODES]


def shift_y(d):
    return [(h * 4 + y, h * 4 + (y + d) % NY) for h in range(2) for y in range(NY)]


def step_of(mantissa, exponent):
    return mantissa * jnp.exp2(exponent)


def encode(sums, count):
    top = jnp.maximum(jnp.max(jnp.abs(sums), axis=0, keepdims=True), 1e-25) * (1.0 / TOP)
    exponent = jnp.floor(jnp.log2(top)) - 13.0
    mantissa = jnp.ceil(top * jnp.exp2(-exponent))
    coded = jnp.round(sums * (1.0 / step_of(mantissa, exponent))).astype(jnp.int32).astype(jnp.int16)
    row = lax.broadcasted_iota(jnp.int32, (16, BLK), 0)
    tail = jnp.where(row == 0, count, jnp.where(row == 1, exponent, jnp.where(row == 2, mantissa, 0.0)))
    return coded, tail.astype(jnp.int32).astype(jnp.int16)


def put_coded(ref, sums, count):
    rows = sums.shape[0]
    coded, tail = encode(sums, count)
    ref[pl.ds(0, rows), :] = coded
    ref[pl.ds(rows, 16), :] = tail


def put_plain(ref, sums, count):
    rows = sums.shape[0]
    ref[pl.ds(0, rows), :] = sums
    ref[pl.ds(rows, 8), :] = jnp.broadcast_to(count, (8, BLK))


def plain(ref):
    rows = ref.shape[0] - 8
    return ref[pl.ds(0, rows), :], ref[pl.ds(rows, 8), :][0:1]


def decode(ref):
    rows = ref.shape[0] - 16
    tail = ref[pl.ds(rows, 16), :].astype(jnp.int32).astype(jnp.float32)
    values = ref[pl.ds(0, rows), :].astype(jnp.int32).astype(jnp.float32)
    return values * step_of(tail[2:3], tail[1:2]), tail[0:1]


def gathered(plain_refs, coded_refs):
    pairs = [plain(ref) for ref in plain_refs] + [decode(ref) for ref in coded_refs]
    return sum(pair[0] for pair in pairs), sum(pair[1] for pair in pairs)


def half_kernel(side_ref, features_ref, out_ref, held, came, went):
    parts = came.shape[0]
    step = held.shape[0] // parts
    cols = pl.ds(pl.multiple_of(side_ref[0] * HALF, HALF), HALF)
    take, give = [], []
    for part in range(parts):
        rows = pl.ds(part * step, step)
        take.append(pltpu.make_async_copy(features_ref.at[rows, cols], held.at[rows, :], came.at[part]))
        give.append(pltpu.make_async_copy(held.at[rows, :], out_ref.at[rows, :], went.at[part]))
    for copy in take:
        copy.start()
    for part in range(parts):
        take[part].wait()
        give[part].start()
    for copy in give:
        copy.wait()


def half_columns(side, features):
    nodes = features.shape[0]
    return pl.pallas_call(
        half_kernel,
        out_shape=jax.ShapeDtypeStruct((nodes, HALF), features.dtype),
        in_specs=[SMEM, pl.BlockSpec(memory_space=pl.ANY)],
        out_specs=pl.BlockSpec(memory_space=pl.ANY),
        scratch_shapes=[pltpu.VMEM((nodes, HALF), features.dtype)] + [pltpu.SemaphoreType.DMA((8,))] * 2,
        compiler_params=ALONE,
        name="half_columns",
    )(side, features)


def sums_kernel(d, pos_ref, table_ref, pat0_ref, pat1_ref, feat0_ref, feat1_ref, even_ref, odd_ref, *scratch):
    tiles, accs, pops, pats, feats, done = scratch[0:2], scratch[2:4], scratch[4:7], scratch[7:9], scratch[9:11], scratch[11]
    blocks = pats[0].shape[0]
    first = lax.rem(pos_ref[0] + d, NX) * blocks
    group = pl.ds(first, blocks)
    half = pl.ds(pl.multiple_of(pos_ref[2] * HALF, HALF), HALF)
    copies = [
        pltpu.make_async_copy(pat0_ref.at[group], pats[0], done.at[0]),
        pltpu.make_async_copy(pat1_ref.at[group], pats[1], done.at[1]),
        pltpu.make_async_copy(feat0_ref.at[:, half], feats[0], done.at[2]),
        pltpu.make_async_copy(feat1_ref, feats[1], done.at[3]),
    ]
    for copy in copies:
        copy.start()
    copies[0].wait()
    copies[1].wait()
    slots = [(side, slot) for side in range(2) for slot in range(FAN)]
    put = put_coded if d else put_plain

    def unpack(i, tile_ref, pop_ref):
        shifts = lax.broadcasted_iota(jnp.int32, (8, 16, BLK), 1)
        total = jnp.zeros((8, BLK), jnp.int32)
        for j, (side, slot) in enumerate(slots):
            live = table_ref[side * 32 + first + i]
            words = pats[side][i, slot] * (slot < live).astype(jnp.int32)
            total += lax.population_count(words)
            bits = (jnp.broadcast_to(words[:, None, :], (8, 16, BLK)) >> shifts) & 1
            tile_ref[pl.ds(j * BLK, BLK), :] = bits.reshape(BLK, BLK).astype(jnp.float32).astype(jnp.bfloat16)
        pop_ref[...] = total

    def multiply(i, tile_ref, acc_ref):
        picked = []
        for side, slot in slots:
            source = table_ref[64 + (side * 32 + first + i) * FAN + slot]
            picked.append(feats[side][pl.ds(pl.multiple_of(source * BLK, BLK), BLK), :])
        acc_ref[...] = F32(tile_ref[...], jnp.concatenate(picked, axis=0), (((0,), (0,)), ((), ()))).T

    def finish(i, acc_ref, pop_ref):
        count = jnp.sum(pop_ref[...], axis=0, keepdims=True).astype(jnp.float32)
        put((even_ref, odd_ref)[i % 2].at[i // 2], acc_ref[...], count)

    for step in range(blocks + 2):
        if step < blocks:
            unpack(step, tiles[step % 2], pops[step % 3])
        if step == 0:
            copies[2].wait()
            copies[3].wait()
        if 0 <= step - 1 < blocks:
            multiply(step - 1, tiles[(step - 1) % 2], accs[(step - 1) % 2])
        if 0 <= step - 2 < blocks:
            finish(step - 2, accs[(step - 2) % 2], pops[(step - 2) % 3])


def sums(d, pos, table, pat0, pat1, feat0, feat1):
    blocks = 2 * NZ
    rows, kind = (HALF + 16, jnp.int16) if d else (HALF + 8, jnp.float32)
    nodes = feat0.shape[0]
    return pl.pallas_call(
        functools.partial(sums_kernel, d),
        out_shape=[jax.ShapeDtypeStruct((NZ, rows, BLK), kind)] * 2,
        in_specs=[SMEM] * 2 + [pl.BlockSpec(memory_space=pl.ANY)] * 4,
        out_specs=[VMEM] * 2,
        scratch_shapes=[pltpu.VMEM((2 * FAN * BLK, BLK), jnp.bfloat16)] * 2
        + [pltpu.VMEM((HALF, BLK), jnp.float32)] * 2
        + [pltpu.VMEM((8, BLK), jnp.int32)] * 3
        + [pltpu.VMEM((blocks,) + pat0.shape[1:], jnp.int32)] * 2
        + [pltpu.VMEM((nodes, HALF), jnp.bfloat16)] * 2
        + [pltpu.SemaphoreType.DMA((4,))],
        compiler_params=ALONE,
        cost_estimate=pl.CostEstimate(flops=2_000_000_000, bytes_accessed=3_000_000, transcendentals=0),
        name="sums",
    )(pos, table, pat0, pat1, feat0, feat1)


def call(kernel, name, outs, count, scratch=(), waits=0, params=PARAMS):
    return pl.pallas_call(
        kernel,
        out_shape=outs,
        in_specs=[SMEM] + [VMEM] * count + [pl.BlockSpec(memory_space=pl.ANY)] * waits,
        out_specs=[VMEM] * len(outs),
        scratch_shapes=list(scratch),
        compiler_params=params,
        name=name,
    )


def shaped(*dims):
    return jax.ShapeDtypeStruct(dims[:-1], dims[-1])


SUM_CODED = shaped(2, HALF + 16, BLK, jnp.int16)
SUM_PLAIN = shaped(2, HALF + 8, BLK, jnp.float32)
CODED = shaped(HALF + 16, BLK, jnp.int16)
PLAIN = shaped(HALF + 8, BLK, jnp.float32)
HALF16 = shaped(HALF, BLK, jnp.bfloat16)


def merge_x_kernel(pos_ref, *rest):
    for step, out_ref in enumerate(rest[-4:]):
        @pl.when(pl.program_id(0) == step)
        def _():
            for c in range(2):
                total, count = gathered((rest[6 + c].at[0],), [ref.at[0] for ref in rest[c:6:2]])
                (put_coded if step else put_plain)(out_ref.at[c], total, count)


def merge_x(pos, *parts):
    block = lambda rows: pl.BlockSpec((1, rows, BLK), lambda d, p: (lax.rem(p[1] + d, NZ), 0, 0))
    outs = [SUM_PLAIN] + [SUM_CODED] * 3
    return pl.pallas_call(
        merge_x_kernel,
        out_shape=outs,
        grid_spec=pltpu.PrefetchScalarGridSpec(
            num_scalar_prefetch=1,
            grid=(NZ,),
            in_specs=[block(part.shape[1]) for part in parts],
            out_specs=[pl.BlockSpec(out.shape, lambda d, p: (0, 0, 0)) for out in outs],
        ),
        compiler_params=ALONE,
        name="merge_x",
    )(pos, *parts)


def merge_z_kernel(pos_ref, r1_ref, r2_ref, r3_ref, own_ref, *rest):
    mine_ref, give_ref, rest_ref = rest[-3:]
    core = pos_ref[2]
    for out_ref, index in ((mine_ref, core), (give_ref, 1 - core)):
        total, count = gathered((own_ref.at[index],), [ref.at[index] for ref in (r1_ref, r2_ref, r3_ref)])
        out_ref[pl.ds(0, HALF), :] = (total / jnp.sqrt(1.0 + count)).astype(jnp.bfloat16)
    for block in range(HALF // 32):
        keep = pl.ds(pl.multiple_of(block * 32 + core * 16, 16), 16)
        give = pl.ds(pl.multiple_of(block * 32 + 16 - core * 16, 16), 16)
        give_ref[pl.ds(HALF + block * 16, 16), :] = mine_ref[give, :]
        rest_ref[pl.ds(block * 16, 16), :] = give_ref[keep, :]


def pre_kernel(
    pos_ref, mine_ref, got_ref, rest_ref, w_ref, self_ref, own_ref, o1_ref, o2_ref, o3_ref, agg0_ref, agg1_ref, agg, acc
):
    core = pos_ref[2]
    agg[pl.ds(pl.multiple_of(core * HALF, HALF), HALF), :] = mine_ref[...]
    agg[pl.ds(pl.multiple_of((1 - core) * HALF, HALF), HALF), :] = got_ref[pl.ds(0, HALF), :]
    acc[...] = (self_ref[...] + F32(agg[...], w_ref[...], (((0,), (0,)), ((), ())))).T
    for d, out_ref in enumerate((own_ref, o1_ref, o2_ref, o3_ref)):
        terms = acc[pl.ds(pl.multiple_of(lax.rem(pos_ref[3] + d, NY) * HALF, HALF), HALF), :]
        (put_coded if d else put_plain)(out_ref, terms, jnp.zeros((1, BLK), jnp.float32))
    for block in range(WIDE // 32):
        rows = pl.ds(pl.multiple_of(block * 32 + core * 16, 16), 16)
        agg0_ref[pl.ds(block * 16, 16), :] = agg[rows, :]
    agg1_ref[pl.ds(pl.multiple_of(core * BLK, BLK), BLK), :] = rest_ref[...]
    agg1_ref[pl.ds(pl.multiple_of((1 - core) * BLK, BLK), BLK), :] = got_ref[pl.ds(HALF, BLK), :]


def merge_y_kernel(pos_ref, r1_ref, r2_ref, r3_ref, own_ref, out_ref):
    total, count = gathered((own_ref,), (r1_ref, r2_ref, r3_ref))
    put_coded(out_ref, total, count)


def hidden_kernel(pos_ref, own_ref, far_ref, out_ref):
    out_ref[...] = jnp.maximum(decode(own_ref)[0] + decode(far_ref)[0], 0.0).astype(jnp.bfloat16)


def grads_kernel(
    pos_ref, a0_ref, a1_ref, a2_ref, a3_ref, b0_ref, b1_ref, b2_ref, b3_ref, og0_ref, og1_ref,
    agg0_ref, agg1_ref, seed0_ref, seed1_ref,
    hidden_ref, own_ref, o1_ref, o2_ref, o3_ref, rows, self_acc, neigh_acc, bias,
):
    x, y = pos_ref[0], pos_ref[3]
    zero = jnp.zeros((BLK, HALF), jnp.bfloat16)
    for d in range(NY):
        place = pl.ds(pl.multiple_of(lax.rem(y + NY - d, NY) * HALF, HALF), HALF)
        for side, (refs, og_ref) in enumerate(
            (((a0_ref, a1_ref, a2_ref, a3_ref), og0_ref), ((b0_ref, b1_ref, b2_ref, b3_ref), og1_ref))
        ):
            value = refs[d][...].T
            if side == 0:
                hidden_ref[:, place] = value
            rows[pl.ds(side * BLK, BLK), place] = jnp.where(value > 0, og_ref[:, place], zero)
    hid = rows.shape[1]
    contract = (((1,), (0,)), ((), ()))
    self_acc[...] = F32(jnp.concatenate([seed0_ref[...], seed1_ref[...]], axis=1), rows[...], contract)
    neigh_acc[...] = F32(jnp.concatenate([agg0_ref[...], agg1_ref[...]], axis=1), rows[...], contract)
    total = F32(jnp.ones((8, 2 * BLK), jnp.bfloat16), rows[...], contract)[0:1]
    for part in range(hid // BLK):
        bias[pl.ds(part, 1), :] = total[:, part * BLK:(part + 1) * BLK]
    row = lax.broadcasted_iota(jnp.int32, (16, BLK), 0)
    for d, out_ref in enumerate((own_ref, o1_ref, o2_ref, o3_ref)):
        to = lax.rem(x + d, NX)
        take = pl.ds(pl.multiple_of(to * 64, 64), 64)
        out_ref[pl.ds(0, 64), pl.ds(0, hid)] = self_acc[take, :].astype(out_ref.dtype)
        out_ref[pl.ds(64, 64), pl.ds(0, hid)] = neigh_acc[take, :].astype(out_ref.dtype)
        left, right = bias[pl.ds(to * 2, 1), :], bias[pl.ds(to * 2 + 1, 1), :]
        left_top = left.astype(jnp.bfloat16).astype(jnp.float32)
        right_top = right.astype(jnp.bfloat16).astype(jnp.float32)
        mark = jnp.where(row == 0, left_top, jnp.where(row == 1, right_top, 0.0))
        mark = jnp.where(row == 2, left - left_top, jnp.where(row == 3, right - right_top, mark))
        out_ref[pl.ds(0, 16), pl.ds(hid, BLK)] = mark.astype(out_ref.dtype)
        out_ref[pl.ds(16, 112), pl.ds(hid, BLK)] = jnp.zeros((112, BLK), out_ref.dtype)


def fold_x_kernel(pos_ref, r1_ref, r2_ref, r3_ref, own_ref, kept_ref, o1_ref, o2_ref, o3_ref, total, bias):
    hid = total.shape[1]
    body, marks = pl.ds(0, hid), pl.ds(hid, BLK)
    refs = (r1_ref, r2_ref, r3_ref)
    total[...] = own_ref[:, body] + sum(ref[:, body].astype(jnp.float32) for ref in refs)
    top = pl.ds(0, 16)
    mark = own_ref[top, marks] + sum(ref[top, marks].astype(jnp.float32) for ref in refs)
    bias[pl.ds(0, 1), :] = mark[0:1] + mark[2:3]
    bias[pl.ds(1, 1), :] = mark[1:2] + mark[3:4]
    row = lax.broadcasted_iota(jnp.int32, (16, BLK), 0)
    for d, out_ref in enumerate((kept_ref, o1_ref, o2_ref, o3_ref)):
        to = lax.rem(pos_ref[1] + d, NZ)
        for kind in range(2):
            take = pl.ds(pl.multiple_of(kind * 64 + to * 16, 16), 16)
            out_ref[pl.ds(kind * 16, 16), body] = total[take, :].astype(out_ref.dtype)
        line = bias[pl.ds(to // 2, 1), :]
        high = line.astype(jnp.bfloat16).astype(jnp.float32)
        mark = jnp.where(row == 0, high, jnp.where(row == 1, line - high, 0.0))
        out_ref[top, marks] = mark.astype(out_ref.dtype)
        out_ref[pl.ds(16, 16), marks] = jnp.zeros((16, BLK), out_ref.dtype)


def last_kernel(pos_ref, r1_ref, r2_ref, r3_ref, own_ref, self_ref, neigh_ref, bias_ref):
    hid = self_ref.shape[1]
    body, marks = pl.ds(0, hid), pl.ds(hid, BLK)
    refs = (r1_ref, r2_ref, r3_ref)
    total = own_ref[:, body] + sum(ref[:, body].astype(jnp.float32) for ref in refs)
    top = pl.ds(0, 16)
    mark = own_ref[top, marks] + sum(ref[top, marks].astype(jnp.float32) for ref in refs)
    self_ref[...] = total[:16]
    neigh_ref[...] = total[16:]
    line = mark[0:1] + mark[1:2]
    for place in range(BLK // 32):
        @pl.when(lax.rem(pos_ref[1], 2) * 2 + pos_ref[2] == place)
        def _():
            bias_ref[...] = line[:, place * 32:place * 32 + 32]


def body(features, seed_feats, patterns, sources, counts, w_self, w_neigh, bias_term, out_grad):
    node = lax.axis_index("node")
    feat = lax.axis_index("feat")
    x, z, core = node // (NZ * 2), (node // 2) % NZ, node % 2
    y = feat % NY
    pos = jnp.stack([x, z, core, y]).astype(jnp.int32)
    hid = w_self.shape[1]
    swap = lambda value: lax.ppermute(value, "node", SWAP_CORE)

    packed = patterns.transpose(0, 1, 3, 2)
    table = jnp.concatenate([counts, sources.reshape(-1)])
    packed_other, table_other = swap(packed), swap(table)
    other = swap(half_columns((1 - core)[None].astype(jnp.int32), features))
    lists = counts.shape[0]
    table = jnp.concatenate([table[:lists], table_other[:lists], table[lists:], table_other[lists:]])

    made = {}
    for d in (2, 1, 3, 0):
        made[d] = sums(d, pos, table, packed, packed_other, features, other)
    far = [lax.ppermute(part, "node", shift_x(d)) for d in (2, 1, 3) for part in made[d]]

    seed_feats, w_self, bias_term, out_grad, own = lax.optimization_barrier(
        (seed_feats, w_self, bias_term, out_grad, made[0])
    )
    turned = seed_feats.T.reshape(WIDE // 32, 2, 16, BLK)
    pick = lambda c: lax.dynamic_index_in_dim(turned, c, 1, keepdims=False).reshape(HALF, BLK)
    seed_mine, seed_other = pick(core), swap(pick(1 - core))
    og_other = swap(out_grad)
    self_term = jnp.dot(seed_feats, w_self, preferred_element_type=jnp.float32)
    self_term = self_term + jnp.where(feat == 0, bias_term, 0.0)

    own, *coded = merge_x(pos, *far, *own)
    arrived = [lax.ppermute(coded[d - 1], "node", shift_z(d)) for d in (2, 1, 3)]
    mine, give, rest = call(
        merge_z_kernel, "merge_z", [HALF16, shaped(HALF + BLK, BLK, jnp.bfloat16), shaped(BLK, BLK, jnp.bfloat16)], 4
    )(pos, *arrived, own)

    *coded, agg_mine, agg_other = call(
        pre_kernel, "pre_terms", [PLAIN] + [CODED] * 3 + [HALF16] * 2, 5,
        [pltpu.VMEM((WIDE, BLK), jnp.bfloat16), pltpu.VMEM((hid, BLK), jnp.float32)],
    )(pos, mine, swap(give), rest, w_neigh, self_term)
    own, *coded = coded
    received = [lax.ppermute(coded[d - 1], "feat", shift_y(d)) for d in (2, 1, 3)]
    (coded,) = call(merge_y_kernel, "merge_y", [CODED], 4)(pos, *received, own)
    far = lax.ppermute(coded, "feat", SWAP_FAR)
    (own,) = call(hidden_kernel, "hidden", [HALF16], 2)(pos, coded, far)
    chunks = [own] + [lax.ppermute(own, "feat", shift_y(d)) for d in (1, 2, 3)]
    chunks_other = [swap(chunk) for chunk in chunks]

    wide = hid + BLK
    scratch = [
        pltpu.VMEM((2 * BLK, hid), jnp.bfloat16),
        pltpu.VMEM((HALF, hid), jnp.float32),
        pltpu.VMEM((HALF, hid), jnp.float32),
        pltpu.VMEM((8, BLK), jnp.float32),
    ]
    outs = [shaped(BLK, hid, jnp.bfloat16), shaped(BLK, wide, jnp.float32)] + [shaped(BLK, wide, jnp.bfloat16)] * 3
    hidden, own, *parts = call(grads_kernel, "grads", outs, 14, scratch)(
        pos, *chunks, *chunks_other, out_grad, og_other, agg_mine, agg_other, seed_mine, seed_other
    )
    received = [lax.ppermute(parts[d - 1], "node", shift_x(d)) for d in (2, 1, 3)]
    own, *parts = call(
        fold_x_kernel, "fold_x", [shaped(32, wide, jnp.float32)] + [shaped(32, wide, jnp.bfloat16)] * 3, 4,
        [pltpu.VMEM((BLK, hid), jnp.float32), pltpu.VMEM((8, BLK), jnp.float32)],
    )(pos, *received, own)
    received = [lax.ppermute(parts[d - 1], "node", shift_z(d)) for d in (2, 1, 3)]
    part = shaped(16, hid, jnp.float32)
    grad_self, grad_neigh, bias = call(last_kernel, "last", [part, part, shaped(1, 32, jnp.float32)], 4)(
        pos, *received, own
    )
    return (hidden, grad_self, grad_neigh, bias[0])


def solution(mesh):
    return jax.shard_map(
        body,
        mesh=mesh,
        in_specs=(
            P("node", "feat"),
            P("node", "feat"),
            P("node", None, None, None),
            P("node", None),
            P("node"),
            P("feat", None),
            P("feat", None),
            P(),
            P("node", None),
        ),
        out_specs=(
            P("node", None),
            P(("feat", "node"), None),
            P(("feat", "node"), None),
            P("node"),
        ),
        check_vma=False,
    )
```
